256 devices in a mesh: group: 4 (over y), region: 64 (over x, z, core).
Axes of the slice: x: 4, y: 4, z: 8, core: 2. Of those that a mesh axis runs over, the one named last changes fastest.
Arguments:
- position: float32 [3, 262144], P(None, ('group', 'region')), may hold values from -6 to 6
- velocity: float32 [3, 262144], P(None, ('group', 'region')), may hold values from -6 to 6
- accel_old: float32 [3, 262144], P(None, ('group', 'region')), may hold values from -6 to 6
- orientation: float32 [9, 262144], P(None, ('group', 'region')), may hold values from -3.5 to 3.5
- spin: float32 [3, 262144], P(None, ('group', 'region')), may hold values from -6 to 6
- shape_index: int32 [262144], P(('group', 'region')), may hold values from 0 to 63
- shape_offsets: float32 [64, 3, 128], replicated, may hold values from -3 to 3
- shape_radii: float32 [64, 128], replicated, may hold values from 0.2 to 0.6
- pair_first: int32 [32768], P(('group', 'region')), may hold values from 0 to 1023
- pair_second: int32 [32768], P(('group', 'region')), may hold values from 0 to 1278
- pair_neck: float32 [32768], P(('group', 'region')), may hold values from 0.05 to 0.5
- cross_first: int32 [16384], P(('group', 'region')), may hold values from 0 to 1023
- cross_second: int32 [16384], P(('group', 'region')), may hold values from 0 to 127
- cross_neck: float32 [16384], P(('group', 'region')), may hold values from 0.05 to 0.5
- export_slots: int32 [32768], P(('group', 'region')), may hold values from 0 to 1023
Outputs:
- moved: float32 [3, 262144], P(None, ('group', 'region'))
- velocity_new: float32 [3, 262144], P(None, ('group', 'region'))
- spin_new: float32 [3, 262144], P(None, ('group', 'region'))
The draws below stay inside these ranges and needn't reach their ends.
All inputs are finite; a program needn't handle non-finite values.
Results may differ from the reference program's by a relative error of at most 0.00002.
Values sent between devices are 32-bit elements; how exact they have to be, the bound alone decides.
No kernel may reach another device: no remote copies, remote signals or barrier semaphores. Data moves between devices by JAX's collectives and lax.ppermute only.
A program may use at most 64 MiB of HBM per device.

```python
import math
import jax
import jax.numpy as jnp
from jax import lax

SUB = 128
SHAPES = 64
G_DEV = 1024
BOUND_DEV = 128
P_DEV = 128
Q_DEV = 64
CX = 32
GRAINS = 262144
PAIRS = 32768
CROSS = 16384
EXPORTS = 32768
N_GROUP = 4
N_REGION = 64


def set_ends(entries, key, least, top_value):
    spot = [jax.random.randint(jax.random.fold_in(key, axis), (), 0, length) for axis, length in enumerate(entries.shape)]
    widest = entries.shape.index(max(entries.shape))
    beside = spot[:widest] + [(spot[widest] + 1) % entries.shape[widest]] + spot[widest + 1:]
    return entries.at[tuple(spot)].set(least).at[tuple(beside)].set(top_value)


def block_levels(rng, extent, cuts, least, top_value):
    def one(dim, parts):
        heights = jax.random.uniform(jax.random.fold_in(jax.random.fold_in(rng, 6), dim), (parts,), jnp.float32, least / len(cuts), top_value / len(cuts))
        return jnp.repeat(jnp.exp(heights), extent[dim] // parts).reshape((-1,) + (1,) * (len(extent) - dim - 1))

    gain = one(*cuts[0])
    for cut in cuts[1:]:
        gain = gain * one(*cut)
    return gain


def normal_values(stream_key, shape, scale, most, split=(), kind=jnp.bfloat16):
    entries = scale * jax.random.normal(stream_key, shape, jnp.float32)
    if split:
        entries = entries * block_levels(stream_key, shape, split, -0.22, 0.18)
    return jnp.clip(entries, -most, most).astype(kind)


def setup_inputs(seed: int = 0) -> dict:
    key_list = jax.random.split(jax.random.key(seed), 16)
    position = normal_values(key_list[0], (3, GRAINS), 1.0, 6.0, ((1, 256),), jnp.float32)
    velocity = normal_values(key_list[1], (3, GRAINS), 1.0, 6.0, ((1, 256),), jnp.float32)
    accel_old = normal_values(key_list[2], (3, GRAINS), 1.0, 6.0, ((1, 256),), jnp.float32)
    orientation = normal_values(key_list[3], (9, GRAINS), 0.6, 3.5, ((1, 256),), jnp.float32)
    spin = normal_values(key_list[4], (3, GRAINS), 1.0, 6.0, ((1, 256),), jnp.float32)
    shape_index = set_ends(jax.random.randint(key_list[5], (GRAINS,), 0, SHAPES), jax.random.fold_in(key_list[5], 1), 0, SHAPES - 1).astype(jnp.int32)
    shape_offsets = normal_values(key_list[6], (SHAPES, 3, SUB), 0.5, 3.0, (), jnp.float32)
    shape_radii = jnp.clip(jax.random.uniform(key_list[7], (SHAPES, SUB), jnp.float32, 0.2, 0.6), 0.2, 0.6)
    pair_first = set_ends(jax.random.randint(key_list[8], (PAIRS,), 0, G_DEV), jax.random.fold_in(key_list[8], 1), 0, G_DEV - 1).astype(jnp.int32)
    pair_second = set_ends(jax.random.randint(key_list[9], (PAIRS,), 0, G_DEV + 2 * BOUND_DEV - 1), jax.random.fold_in(key_list[9], 1), 0, (G_DEV + 2 * BOUND_DEV - 1) - 1).astype(jnp.int32)
    pair_neck = jnp.clip(jnp.exp(math.log(0.5) - 2.3025851 * jax.random.uniform(key_list[10], (PAIRS,), jnp.float32) ** block_levels(key_list[10], (PAIRS,), ((0, 256),), -0.2, 0.2)), 0.05, 0.5)
    cross_first = set_ends(jax.random.randint(key_list[11], (CROSS,), 0, G_DEV), jax.random.fold_in(key_list[11], 1), 0, G_DEV - 1).astype(jnp.int32)
    cross_second = set_ends(jax.random.randint(key_list[12], (CROSS,), 0, N_GROUP * CX), jax.random.fold_in(key_list[12], 1), 0, (N_GROUP * CX) - 1).astype(jnp.int32)
    cross_neck = jnp.clip(jnp.exp(math.log(0.5) - 2.3025851 * jax.random.uniform(key_list[13], (CROSS,), jnp.float32) ** block_levels(key_list[13], (CROSS,), ((0, 256),), -0.2, 0.2)), 0.05, 0.5)
    export_slots = set_ends(jax.random.randint(key_list[14], (EXPORTS,), 0, G_DEV), jax.random.fold_in(key_list[14], 1), 0, G_DEV - 1).astype(jnp.int32)
    return dict(position=position, velocity=velocity, accel_old=accel_old, orientation=orientation, spin=spin, shape_index=shape_index, shape_offsets=shape_offsets, shape_radii=shape_radii, pair_first=pair_first, pair_second=pair_second, pair_neck=pair_neck, cross_first=cross_first, cross_second=cross_second, cross_neck=cross_neck, export_slots=export_slots)


time_step = 0.05
stiffness = 0.0078125
cohesion = 0.05
inertia = 0.4

def build(centre, turn, chosen):
    offsets = chosen[:, :3]
    rows = []
    for c in range(3):
        value = centre[c][:, None] + turn[3 * c][:, None] * offsets[:, 0]
        value = value + turn[3 * c + 1][:, None] * offsets[:, 1]
        value = value + turn[3 * c + 2][:, None] * offsets[:, 2]
        rows.append(value)
    rows.append(chosen[:, 3])
    return jnp.stack(rows, 1)

def crossed(left, right):
    return jnp.stack([left[:, 1] * right[:, 2] - left[:, 2] * right[:, 1], left[:, 2] * right[:, 0] - left[:, 0] * right[:, 2], left[:, 0] * right[:, 1] - left[:, 1] * right[:, 0]], 1)

def tile(world_i, centre_i, world_j, centre_j, neck):
    delta = world_i[:, :3, :, None] - world_j[:, :3, None, :]
    square = delta[:, 0] ** 2 + delta[:, 1] ** 2 + delta[:, 2] ** 2
    spacing = jnp.sqrt(square + 0.01)
    reach = world_i[:, 3, :, None] + world_j[:, 3, None, :]
    magnitude = (stiffness * (reach - spacing) - cohesion * neck[:, None, None]) * jnp.exp(-square * 0.25) / spacing
    pushes = magnitude[:, None] * delta
    along_i = lax.optimization_barrier(jnp.sum(pushes, 3))
    along_j = lax.optimization_barrier(jnp.sum(pushes, 2))
    force_i = lax.optimization_barrier(jnp.sum(along_i, 2))
    torque_i = lax.optimization_barrier(jnp.sum(crossed(world_i[:, :3] - centre_i[:, :, None], along_i), 2))
    torque_j = -lax.optimization_barrier(jnp.sum(crossed(world_j[:, :3] - centre_j[:, :, None], along_j), 2))
    return (jnp.concatenate([force_i, torque_i], 1), jnp.concatenate([-force_i, torque_j], 1))

def reference(position, velocity, accel_old, orientation, spin, shape_index, shape_offsets, shape_radii, pair_first, pair_second, pair_neck, cross_first, cross_second, cross_neck, export_slots):
    moved = position + time_step * velocity + 0.5 * time_step ** 2 * accel_old
    table = jnp.concatenate([shape_offsets, shape_radii[:, None, :]], 1)
    device = jnp.arange(PAIRS, dtype=jnp.int32) // P_DEV
    group = device // N_REGION
    region = device % N_REGION
    first_a = device * G_DEV + pair_first
    local_b = device * G_DEV + (pair_first + 1 + pair_second) % G_DEV
    rest = pair_second - (G_DEV - 1)
    near_region = (region - 1 + 2 * (rest // BOUND_DEV) + N_REGION) % N_REGION
    far_b = (group * N_REGION + near_region) * G_DEV + rest % BOUND_DEV
    second_a = jnp.where(pair_second < G_DEV - 1, local_b, far_b)
    device = jnp.arange(CROSS, dtype=jnp.int32) // Q_DEV
    group = device // N_REGION
    source = cross_second // CX * N_REGION + device % N_REGION
    slot = export_slots[source * (N_GROUP * CX) + group * CX + cross_second % CX]
    first_b = device * G_DEV + cross_first
    second_b = source * G_DEV + slot
    firsts = jnp.concatenate([first_a, first_b]).astype(jnp.int32)
    seconds = jnp.concatenate([second_a, second_b]).astype(jnp.int32)
    necks = jnp.concatenate([pair_neck, cross_neck])
    total = PAIRS + CROSS
    block = math.gcd(total, 64)

    def world_of(index):
        centre = moved[:, index]
        return (build(centre, orientation[:, index], table[shape_index[index]]), centre.T)

    def work(pieces):
        one, two, neck = pieces
        world_i, centre_i = world_of(one)
        world_j, centre_j = world_of(two)
        return tile(world_i, centre_i, world_j, centre_j, neck)
    terms_i, terms_j = lax.map(work, (firsts.reshape(-1, block), seconds.reshape(-1, block), necks.reshape(-1, block)))
    totals = jax.ops.segment_sum(terms_i.reshape(total, 6), firsts, num_segments=GRAINS)
    totals = totals + jax.ops.segment_sum(terms_j.reshape(total, 6), seconds, num_segments=GRAINS)
    force = totals[:, :3].T
    torque = totals[:, 3:].T
    velocity_new = velocity + 0.5 * time_step * (accel_old + force)
    spin_new = spin + time_step * torque / inertia
    return (moved, velocity_new, spin_new)
```

```python
import functools
import math

import jax
import jax.numpy as jnp
from jax import lax
from jax.experimental import pallas as pl
from jax.experimental.pallas import tpu as pltpu
from jax.sharding import PartitionSpec as P

F32 = jnp.float32
BF16 = jnp.bfloat16
I32 = jnp.int32

BOUND_DEV = 128
CX = 32
KINDS = 64
SUB = 128
GRAINS_DEV = 1024
LANES = 128
UNIT = 32
PARTS = LANES // UNIT
ROWS = SUB // PARTS

time_step = 0.05
stiffness = 0.0078125
cohesion = 0.05
inertia = 0.4

SCALE = math.sqrt(math.log2(math.e) / 4)
SOFT = 0.01 * SCALE * SCALE
LIFT = 2.0**SOFT
GAIN = LIFT * SCALE * stiffness
BOND = LIFT * SCALE * cohesion
DRAG = LIFT * stiffness


def iota(shape, dim):
    return lax.broadcasted_iota(I32, shape, dim)


def thirds(x):
    hi = x.astype(BF16).astype(F32)
    rest = x - hi
    mid = rest.astype(BF16).astype(F32)
    return jnp.concatenate([hi, mid, rest - mid], 0).astype(BF16)


def joined(y):
    n = y.shape[0] // 3
    return (y[2 * n :] + y[n : 2 * n]) + y[:n]


def dot(a, b):
    return lax.dot_general(a, b, (((1,), (0,)), ((), ())), preferred_element_type=F32)


def dot_t(a, b):
    return lax.dot_general(a, b, (((1,), (1,)), ((), ())), preferred_element_type=F32)


def hot(index, count):
    return jnp.where(iota((count, index.shape[1]), 0) == index, 1.0, 0.0).astype(BF16)


def wide(row):
    return jnp.concatenate([row, jnp.zeros((1, LANES - row.shape[1]), row.dtype)], 1)


def stack(rows, count):
    at = iota((count, rows[0].shape[1]), 0)
    out = jnp.zeros((count, rows[0].shape[1]), F32)
    for k, row in enumerate(rows):
        out = jnp.where(at == k, row, out)
    return out


def compact(actives, fields):
    segments = len(actives)
    flags = stack([a.astype(F32) for a in actives], 16)
    below = jnp.where(iota((LANES, LANES), 0) < iota((LANES, LANES), 1), 1.0, 0.0).astype(BF16)
    inside = dot(flags.astype(BF16), below)
    sums = dot(flags.astype(BF16), jnp.ones((LANES, LANES), BF16))
    ranks = []
    before = jnp.zeros((1, LANES), F32)
    for s in range(segments):
        ranks.append(jnp.where(actives[s], inside[s : s + 1] + before, -1.0).astype(I32))
        before = before + sums[s : s + 1]
    total = jnp.sum(flags).astype(I32)
    parts = thirds(jnp.concatenate([stack(f, 16) for f in fields], 1))
    return jnp.concatenate(ranks, 1), parts, total


def picked(ranks, parts, base):
    want = iota((LANES, ranks.shape[1]), 0) + base
    chosen = jnp.where(want == ranks, 1.0, 0.0).astype(BF16)
    return joined(dot_t(parts, chosen))


def pair_unit(number, pose_ref, table_ref, u_ref, v_ref, both):
    spread = jnp.where(
        iota((LANES, LANES), 0) == number * UNIT + (iota((LANES, LANES), 1) & (UNIT - 1)), 1.0, 0.0
    ).astype(BF16)
    pose = joined(dot(pose_ref[...], spread))
    part = iota((1, LANES), 1) // UNIT
    shift = [SCALE * (pose[c : c + 1] - pose[16 + c : 17 + c]) for c in range(3)]

    def kinds(row):
        at = iota((4 * KINDS, LANES), 0)
        kind = row.astype(I32)
        return jnp.where(((at & (KINDS - 1)) == kind) & (at < 3 * KINDS), 1.0, 0.0).astype(BF16)

    second = dot(table_ref[...], kinds(pose[28:29]))
    for c in range(3):
        turn = [SCALE * pose[16 + 3 + 3 * c + e : 16 + 4 + 3 * c + e] for e in range(3)]
        v_ref[c] = turn[0] * second[:SUB] + turn[1] * second[SUB : 2 * SUB] + turn[2] * second[2 * SUB : 3 * SUB]
    v_ref[3] = GAIN * second[3 * SUB :]

    first = dot(table_ref[...], kinds(pose[12:13]))
    mine = []
    for e in range(4):
        value = first[e * SUB : e * SUB + ROWS]
        for k in range(1, PARTS):
            value = jnp.where(part == k, first[e * SUB + k * ROWS : e * SUB + (k + 1) * ROWS], value)
        mine.append(value)
    for c in range(3):
        turn = [SCALE * pose[3 + 3 * c + e : 4 + 3 * c + e] for e in range(3)]
        u_ref[c] = shift[c] + (turn[0] * mine[0] + turn[1] * mine[1] + turn[2] * mine[2])
    u_ref[3] = GAIN * mine[3] - BOND * pose[13:14]

    blocks = ROWS // 8
    u = [[u_ref[c, 8 * k : 8 * k + 8, :] for c in range(4)] for k in range(blocks)]

    def step(b, sums):
        v = [v_ref[c, pl.ds(b, 8, stride=0), :] for c in range(4)]
        out = []
        for k in range(blocks):
            x, y, z = (u[k][c] - v[c] for c in range(3))
            square = (x * x + SOFT) + y * y + z * z
            m = ((u[k][3] + v[3]) * lax.rsqrt(square) - DRAG) * jnp.exp2(-square)
            s = sums[k]
            out.append((s[0] + m * v[0], s[1] + m * v[1], s[2] + m * v[2], s[3] + m))
        return tuple(out)

    zero = jnp.zeros((8, LANES), F32)
    sums = lax.fori_loop(0, SUB, step, ((zero,) * 4,) * blocks, unroll=4)

    terms = [zero] * 9
    for k in range(blocks):
        z = sums[k][:3]
        g = [sums[k][3] * u[k][c] - z[c] for c in range(3)]
        arm = [u[k][c] - shift[c] for c in range(3)]
        for c in range(3):
            n, o = (c + 1) % 3, (c + 2) % 3
            terms[c] = terms[c] + g[c]
            terms[3 + c] = terms[3 + c] + (arm[n] * g[o] - arm[o] * g[n])
            if both:
                terms[6 + c] = terms[6 + c] - (z[n] * u[k][o] - z[o] * u[k][n])
    rows = [jnp.sum(t, 0, keepdims=True) for t in terms]
    rows = [r * (1 / SCALE if k < 3 else 1 / SCALE**2) for k, r in enumerate(rows)]
    zero_row = jnp.zeros((1, LANES), F32)
    listed = rows[:6] + [zero_row, zero_row]
    if both:
        listed += [-r for r in rows[:3]] + rows[6:]
    return joined(dot_t(thirds(stack(listed, 16)), spread))


def prepare_kernel(
    position_ref, velocity_ref, accel_ref, turn_ref, kind_ref, first_ref, second_ref, neck_ref,
    cross_first_ref, cross_second_ref, cross_neck_ref, export_ref,
    moved_ref, pose_ref, near_ref, far1_ref, far2_ref, far3_ref,
):
    group = lax.axis_index("group")
    moved = position_ref[...] + time_step * velocity_ref[...] + 0.5 * time_step**2 * accel_ref[...]
    moved_ref[...] = moved
    pose_ref[0:3, :] = moved
    pose_ref[3:12, :] = turn_ref[...]
    pose_ref[12:13, :] = kind_ref[...].astype(F32)
    pose_ref[13:16, :] = jnp.zeros((3, GRAINS_DEV), F32)
    index = jnp.concatenate([first_ref[...], wide(cross_first_ref[...]), export_ref[...]], 1)
    got = joined(dot(thirds(pose_ref[...]), hot(index, GRAINS_DEV)))
    at = iota((16, LANES), 0)
    near_ref[0:16, :] = pose_ref[:, :BOUND_DEV]
    listed = jnp.where(at == 13, second_ref[...].astype(F32), got[:, :LANES])
    near_ref[16:32, :] = jnp.where(at == 14, neck_ref[...], listed)
    listed = jnp.where(at == 13, wide(cross_second_ref[...]).astype(F32), got[:, LANES : 2 * LANES])
    listed = jnp.where(at == 14, wide(cross_neck_ref[...]), listed)
    exported = got[:, 2 * LANES :]
    for k, far_ref in ((1, far1_ref), (2, far2_ref), (3, far3_ref)):
        to = (group + k) & 3
        turned = pltpu.roll(exported, (64 - CX * to) & (LANES - 1), 1)
        far_ref[...] = jnp.where(iota((16, LANES), 1) < 64, listed, turned)


def tiles(total, ranks, parts, other_of, poses_ref, table_ref, out_ref, pose_ref, u_ref, v_ref, both):
    def tile(t, carry):
        fields = picked(ranks, parts, t * LANES)
        own = hot(fields[0:1].astype(I32) - 1, GRAINS_DEV)
        mine = joined(dot(poses_ref[...], own))
        mine = jnp.where(iota((16, LANES), 0) == 13, fields[2:3], mine)
        other_index = fields[1:2].astype(I32) - 1
        other = hot(other_index, other_of.shape[1])
        theirs = joined(dot(other_of[...], other))
        pose_ref[...] = thirds(jnp.concatenate([mine, theirs], 0))
        units = jnp.minimum(PARTS, (total - t * LANES + UNIT - 1) // UNIT)
        terms = lax.fori_loop(
            0,
            units,
            lambda n, s: s + pair_unit(n, pose_ref, table_ref, u_ref, v_ref, both),
            jnp.zeros((16, LANES), F32),
        )
        found = joined(dot_t(thirds(terms[:8]), own))
        if both:
            found = found + joined(dot_t(thirds(terms[8:]), other))
        out_ref[...] += found
        return carry

    lax.fori_loop(0, (total + LANES - 1) // LANES, tile, 0)


def local_kernel(
    poses_in_ref, first_ref, second_ref, neck_ref, cross_first_ref, cross_second_ref, cross_neck_ref, export_ref,
    offset_ref, radius_ref,
    out_ref, table_ref,
    poses_ref, pose_ref, u_ref, v_ref,
):
    group = lax.axis_index("group")
    blank = jnp.zeros((LANES - KINDS, SUB), F32)
    for e in range(4):
        rows = radius_ref[...] if e == 3 else offset_ref[:, e, :]
        hi = rows.astype(BF16).astype(F32)
        mid = (rows - hi).astype(BF16).astype(F32)
        low = rows - hi - mid
        table_ref[e * SUB : (e + 1) * SUB, :LANES] = jnp.concatenate([hi, mid], 0).T.astype(BF16)
        table_ref[e * SUB : (e + 1) * SUB, LANES:] = jnp.concatenate([low, blank], 0).T.astype(BF16)
    poses_ref[...] = thirds(poses_in_ref[...])
    out_ref[...] = jnp.zeros_like(out_ref)
    first, second = first_ref[...], second_ref[...]
    cross = wide(cross_second_ref[...])
    ours = (cross >> 5 == group) & (iota((1, LANES), 1) < cross_second_ref.shape[1])
    slot = joined(dot(thirds(stack([export_ref[...].astype(F32)], 16)), hot(cross, LANES)))[0:1]
    partner = (first + 1 + second) & (GRAINS_DEV - 1)
    ranks, parts, total = compact(
        [second < GRAINS_DEV - 1, ours],
        [
            [(first + 1).astype(F32), (partner + 1).astype(F32), neck_ref[...]],
            [(wide(cross_first_ref[...]) + 1).astype(F32), slot + 1, wide(cross_neck_ref[...])],
        ],
    )
    tiles(total, ranks, parts, poses_ref, poses_ref, table_ref, out_ref, pose_ref, u_ref, v_ref, True)


def remote_kernel(
    poses_in_ref, first_ref, second_ref, neck_ref, cross_first_ref, cross_second_ref, cross_neck_ref, export_ref,
    table_ref, local_ref, velocity_ref, accel_ref, spin_ref, before_ref, after_ref, far1_ref, far2_ref, far3_ref,
    velocity_out_ref, spin_out_ref,
    poses_ref, pool_ref, out_ref, pose_ref, u_ref, v_ref,
):
    group = lax.axis_index("group")
    lane = iota((1, LANES), 1)
    poses_ref[...] = thirds(poses_in_ref[...])
    fars = (far1_ref, far2_ref, far3_ref)
    pool = [before_ref[0:16, :], after_ref[0:16, :], before_ref[16:32, :], after_ref[16:32, :]]
    pool_ref[...] = thirds(jnp.concatenate(pool + [f[...] for f in fars], 1))
    out_ref[...] = local_ref[...]
    actives, fields = [], []

    def add(active, own, place, neck):
        actives.append(active)
        fields.append([(own + 1).astype(F32), (place + 1).astype(F32), neck])

    beyond = second_ref[...] - (GRAINS_DEV - 1)
    add(beyond >= 0, first_ref[...], beyond, neck_ref[...])
    cross = wide(cross_second_ref[...])
    way = (group - (cross >> 5)) & 3
    add(
        (way != 0) & (lane < 64),
        wide(cross_first_ref[...]),
        3 * LANES + way * LANES + 64 + (cross & (CX - 1)),
        wide(cross_neck_ref[...]),
    )
    beyond = before_ref[29:30, :].astype(I32) - (GRAINS_DEV - 1)
    add(beyond >= BOUND_DEV, beyond - BOUND_DEV, 2 * LANES + lane, before_ref[30:31, :])
    beyond = after_ref[29:30, :].astype(I32) - (GRAINS_DEV - 1)
    add((beyond >= 0) & (beyond < BOUND_DEV), beyond, 3 * LANES + lane, after_ref[30:31, :])
    exports = thirds(stack([export_ref[...].astype(F32)], 16))
    for k in (1, 2, 3):
        wanted = fars[k - 1][13:14, :].astype(I32)
        sender = (group - k) & 3
        slot = joined(dot(exports, hot(sender * CX + (wanted & (CX - 1)), LANES)))[0:1]
        add(
            (wanted >> 5 == group) & (lane < 64),
            slot,
            (3 + k) * LANES + lane,
            fars[k - 1][14:15, :],
        )
    ranks, parts, total = compact(actives, fields)
    tiles(total, ranks, parts, pool_ref, poses_ref, table_ref, out_ref, pose_ref, u_ref, v_ref, False)
    velocity_out_ref[...] = velocity_ref[...] + 0.5 * time_step * (accel_ref[...] + out_ref[0:3, :])
    spin_out_ref[...] = spin_ref[...] + time_step * out_ref[3:6, :] / inertia


def shifted(array, axis, by):
    devices = lax.axis_size(axis)
    return lax.ppermute(array, axis, [(i, (i + by) % devices) for i in range(devices)])


def shape(rows, columns, kind=F32):
    return jax.ShapeDtypeStruct((rows, columns), kind)


def on_device(
    position, velocity, accel_old, orientation, spin, shape_index, shape_offsets, shape_radii,
    pair_first, pair_second, pair_neck, cross_first, cross_second, cross_neck, export_slots,
):
    row = lambda x: x.reshape(1, x.shape[0])
    lists = [row(x) for x in (pair_first, pair_second, pair_neck, cross_first, cross_second, cross_neck, export_slots)]
    moved, poses, near, far1, far2, far3 = pl.pallas_call(
        prepare_kernel,
        out_shape=(
            shape(3, GRAINS_DEV), shape(16, GRAINS_DEV), shape(32, LANES),
            shape(16, LANES), shape(16, LANES), shape(16, LANES),
        ),
        compiler_params=pltpu.CompilerParams(vmem_limit_bytes=48 << 20),
        name="prepare",
    )(position, velocity, accel_old, orientation, row(shape_index), *lists)
    before = shifted(near, "region", 1)
    after = shifted(near, "region", -1)
    fars = [shifted(f, "group", k) for k, f in ((1, far1), (2, far2), (3, far3))]
    work = [
        pltpu.VMEM((96, LANES), BF16),
        pltpu.VMEM((4, ROWS, LANES), F32),
        pltpu.VMEM((4, SUB, LANES), F32),
    ]
    local, table = pl.pallas_call(
        local_kernel,
        out_shape=(shape(8, GRAINS_DEV), shape(4 * SUB, 4 * KINDS, BF16)),
        scratch_shapes=[pltpu.VMEM((48, GRAINS_DEV), BF16)] + work,
        compiler_params=pltpu.CompilerParams(vmem_limit_bytes=48 << 20),
        cost_estimate=pl.CostEstimate(flops=4_000_000_000, bytes_accessed=1_000_000, transcendentals=4_000_000),
        name="local",
    )(poses, *lists, shape_offsets, shape_radii)
    velocity_new, spin_new = pl.pallas_call(
        remote_kernel,
        out_shape=(shape(3, GRAINS_DEV), shape(3, GRAINS_DEV)),
        scratch_shapes=[
            pltpu.VMEM((48, GRAINS_DEV), BF16), pltpu.VMEM((48, 7 * LANES), BF16), pltpu.VMEM((8, GRAINS_DEV), F32)
        ] + work,
        compiler_params=pltpu.CompilerParams(vmem_limit_bytes=48 << 20),
        name="remote",
    )(poses, *lists, table, local, velocity, accel_old, spin, before, after, *fars)
    return (moved, velocity_new, spin_new)


def solution(mesh):
    both = ("group", "region")
    wide_spec, flat = P(None, both), P(both)
    return jax.shard_map(
        on_device,
        mesh=mesh,
        in_specs=(wide_spec,) * 5 + (flat, P(), P()) + (flat,) * 7,
        out_specs=(wide_spec,) * 3,
        check_vma=False,
    )
```

```python
import functools
import math

import jax
import jax.numpy as jnp
from jax import lax
from jax.experimental import pallas as pl
from jax.experimental.pallas import tpu as pltpu
from jax.sharding import PartitionSpec as P

F32 = jnp.float32
BF16 = jnp.bfloat16
I32 = jnp.int32

BOUND_DEV = 128
CX = 32
KINDS = 64
SUB = 128
GRAINS_DEV = 1024
LANES = 128
UNIT = 32
PARTS = LANES // UNIT
ROWS = SUB // PARTS

time_step = 0.05
stiffness = 0.0078125
cohesion = 0.05
inertia = 0.4

SCALE = math.sqrt(math.log2(math.e) / 4)
SOFT = 0.01 * SCALE * SCALE
LIFT = 2.0**SOFT
GAIN = LIFT * SCALE * stiffness
BOND = LIFT * SCALE * cohesion
DRAG = LIFT * stiffness


def iota(shape, dim):
    return lax.broadcasted_iota(I32, shape, dim)


def thirds(x):
    hi = x.astype(BF16).astype(F32)
    rest = x - hi
    mid = rest.astype(BF16).astype(F32)
    return jnp.concatenate([hi, mid, rest - mid], 0).astype(BF16)


def joined(y):
    n = y.shape[0] // 3
    return (y[2 * n :] + y[n : 2 * n]) + y[:n]


def dot(a, b):
    return lax.dot_general(a, b, (((1,), (0,)), ((), ())), preferred_element_type=F32)


def dot_t(a, b):
    return lax.dot_general(a, b, (((1,), (1,)), ((), ())), preferred_element_type=F32)


def hot(index, count):
    return jnp.where(iota((count, index.shape[1]), 0) == index, 1.0, 0.0).astype(BF16)


def wide(row):
    return jnp.concatenate([row, jnp.zeros((1, LANES - row.shape[1]), row.dtype)], 1)


def stack(rows, count):
    at = iota((count, rows[0].shape[1]), 0)
    out = jnp.zeros((count, rows[0].shape[1]), F32)
    for k, row in enumerate(rows):
        out = jnp.where(at == k, row, out)
    return out


def compact(actives, fields):
    segments = len(actives)
    flags = stack([a.astype(F32) for a in actives], 16)
    below = jnp.where(iota((LANES, LANES), 0) < iota((LANES, LANES), 1), 1.0, 0.0).astype(BF16)
    inside = dot(flags.astype(BF16), below)
    sums = dot(flags.astype(BF16), jnp.ones((LANES, LANES), BF16))
    ranks = []
    before = jnp.zeros((1, LANES), F32)
    for s in range(segments):
        ranks.append(jnp.where(actives[s], inside[s : s + 1] + before, -1.0).astype(I32))
        before = before + sums[s : s + 1]
    total = jnp.sum(flags).astype(I32)
    parts = thirds(jnp.concatenate([stack(f, 16) for f in fields], 1))
    return jnp.concatenate(ranks, 1), parts, total


def picked(ranks, parts, base):
    want = iota((LANES, ranks.shape[1]), 0) + base
    chosen = jnp.where(want == ranks, 1.0, 0.0).astype(BF16)
    return joined(dot_t(parts, chosen))


def quarter_of(lanes, blocks):
    out = blocks[0]
    for h in range(1, PARTS):
        out = jnp.where(lanes == h, blocks[h], out)
    return out


def worlds(table_ref, pose):
    at = iota((4 * KINDS, LANES), 0)
    kinds = jnp.where(((at & (KINDS - 1)) == pose[12:13].astype(I32)) & (at < 3 * KINDS), 1.0, 0.0).astype(BF16)
    shapes = dot(table_ref[...], kinds)
    offset = [shapes[e * SUB : (e + 1) * SUB] for e in range(4)]
    turn = [SCALE * pose[3 + n : 4 + n] for n in range(9)]
    return [
        turn[3 * c] * offset[0] + turn[3 * c + 1] * offset[1] + turn[3 * c + 2] * offset[2] for c in range(3)
    ] + [GAIN * offset[3]]


def turned_copies(ref, item, value):
    ref[item, 0] = value
    for j in range(1, PARTS):
        ref[item, j] = pltpu.roll(value, j * UNIT, 1)


def pair_unit(number, terms, first_ref, second_ref, v_ref, both):
    part = iota((8, LANES), 1) // UNIT
    ways = [(h + PARTS - number) & (PARTS - 1) for h in range(PARTS)]
    blocks = ROWS // 8
    for c in range(4):
        for k in range(SUB // 8):
            v_ref[c, 8 * k : 8 * k + 8, :] = quarter_of(
                part, [second_ref[c, w, 8 * k : 8 * k + 8, :] for w in ways]
            )
    u = [
        [
            quarter_of(part, [first_ref[c, w, h * ROWS + 8 * k : h * ROWS + 8 * k + 8, :] for h, w in enumerate(ways)])
            for c in range(4)
        ]
        for k in range(blocks)
    ]

    def step(b, sums):
        v = [v_ref[c, pl.ds(b, 8, stride=0), :] for c in range(4)]
        out = []
        for k in range(blocks):
            x, y, z = (u[k][c] - v[c] for c in range(3))
            square = (x * x + SOFT) + y * y + z * z
            m = ((u[k][3] + v[3]) * lax.rsqrt(square) - DRAG) * jnp.exp2(-square)
            s = sums[k]
            if both:
                out.append((s[0] + m * v[0], s[1] + m * v[1], s[2] + m * v[2], s[3] + m))
            else:
                out.append((s[0] + m * x, s[1] + m * y, s[2] + m * z))
        return tuple(out)

    zero = jnp.zeros((8, LANES), F32)
    sums = lax.fori_loop(0, SUB, step, ((zero,) * (4 if both else 3),) * blocks, unroll=8)

    rows = [zero] * 9
    for k in range(blocks):
        if both:
            z = sums[k][:3]
            g = [sums[k][3] * u[k][c] - z[c] for c in range(3)]
        else:
            g = sums[k]
        for c in range(3):
            n, o = (c + 1) % 3, (c + 2) % 3
            rows[c] = rows[c] + g[c]
            rows[3 + c] = rows[3 + c] + (u[k][n] * g[o] - u[k][o] * g[n])
            if both:
                rows[6 + c] = rows[6 + c] - (z[n] * u[k][o] - z[o] * u[k][n])
    rows = [jnp.sum(t, 0, keepdims=True) for t in rows]
    found = stack(rows, 16)
    found = found + pltpu.roll(found, 2 * UNIT, 1)
    found = found + pltpu.roll(found, UNIT, 1)
    return jnp.where(iota((16, LANES), 1) // UNIT == number, found, terms)


def prepare_kernel(
    position_hbm, velocity_hbm, accel_hbm, turn_hbm, kind_hbm, first_hbm, second_hbm, neck_hbm,
    cross_first_hbm, cross_second_hbm, cross_neck_hbm, export_hbm,
    moved_ref, pose_ref, list_ref, near_ref, far1_ref, far2_ref, far3_ref,
    position_ref, velocity_ref, accel_ref, turn_ref, kind_ref, first_ref, second_ref, neck_ref,
    cross_first_ref, cross_second_ref, cross_neck_ref, export_ref, sems,
):
    sources = (
        position_hbm, velocity_hbm, accel_hbm, turn_hbm, kind_hbm, first_hbm, second_hbm, neck_hbm,
        cross_first_hbm, cross_second_hbm, cross_neck_hbm, export_hbm,
    )
    targets = (
        position_ref, velocity_ref, accel_ref, turn_ref, kind_ref, first_ref, second_ref, neck_ref,
        cross_first_ref, cross_second_ref, cross_neck_ref, export_ref,
    )
    copies = [pltpu.make_async_copy(a, b, sems.at[k]) for k, (a, b) in enumerate(zip(sources, targets))]
    for copy in copies:
        copy.start()
    for copy in copies:
        copy.wait()
    group = lax.axis_index("group")
    moved = position_ref[...] + time_step * velocity_ref[...] + 0.5 * time_step**2 * accel_ref[...]
    moved_ref[...] = moved
    pose_ref[0:3, :] = moved
    pose_ref[3:12, :] = turn_ref[...]
    pose_ref[12:13, :] = kind_ref[...].astype(F32)
    pose_ref[13:16, :] = jnp.zeros((3, GRAINS_DEV), F32)
    index = jnp.concatenate([first_ref[...], wide(cross_first_ref[...]), export_ref[...]], 1)
    got = joined(dot(thirds(pose_ref[...]), hot(index, GRAINS_DEV)))
    at = iota((16, LANES), 0)
    second, neck = second_ref[...].astype(F32), neck_ref[...]
    cross_second, cross_neck = wide(cross_second_ref[...]).astype(F32), wide(cross_neck_ref[...])
    near_ref[0:16, :] = pose_ref[:, :BOUND_DEV]
    near_ref[16:32, :] = jnp.where(at == 14, neck, jnp.where(at == 13, second, got[:, :LANES]))
    listed = jnp.where(at == 14, cross_neck, jnp.where(at == 13, cross_second, got[:, LANES : 2 * LANES]))
    exported = got[:, 2 * LANES :]
    for k, far_ref in ((1, far1_ref), (2, far2_ref), (3, far3_ref)):
        to = (group + k) & 3
        turned = pltpu.roll(exported, (64 - CX * to) & (LANES - 1), 1)
        far_ref[...] = jnp.where(iota((16, LANES), 1) < 64, listed, turned)
    first, cross_first = first_ref[...].astype(F32), wide(cross_first_ref[...]).astype(F32)
    list_ref[...] = stack(
        [first, second, neck, cross_first, cross_second, cross_neck, export_ref[...].astype(F32)], 8
    )


def tiles(total, ranks, parts, other_of, poses_ref, table_ref, out_ref, u_ref, w_ref, v_ref, both):
    def tile(t, carry):
        fields = picked(ranks, parts, t * LANES)
        own = hot(fields[0:1].astype(I32) - 1, GRAINS_DEV)
        mine = joined(dot(poses_ref[...], own))
        other = hot(fields[1:2].astype(I32) - 1, other_of.shape[1])
        theirs = joined(dot(other_of[...], other))
        shift = [SCALE * (mine[c : c + 1] - theirs[c : c + 1]) for c in range(3)]
        for c, value in enumerate(worlds(table_ref, theirs)):
            turned_copies(w_ref, c, value)
        for c, value in enumerate(worlds(table_ref, mine)):
            turned_copies(u_ref, c, value + shift[c] if c < 3 else value - BOND * fields[2:3])
        units = jnp.minimum(PARTS, (total - t * LANES + UNIT - 1) // UNIT)
        terms = lax.fori_loop(
            0,
            units,
            lambda n, s: pair_unit(n, s, u_ref, w_ref, v_ref, both),
            jnp.zeros((16, LANES), F32),
        )
        force = [terms[c : c + 1] for c in range(3)]
        rows = [f * (1 / SCALE) for f in force]
        for c in range(3):
            n, o = (c + 1) % 3, (c + 2) % 3
            rows.append((terms[3 + c : 4 + c] - (shift[n] * force[o] - shift[o] * force[n])) * (1 / SCALE**2))
        found = joined(dot_t(thirds(stack(rows, 8)), own))
        if both:
            back = [-r for r in rows[:3]] + [terms[6 + c : 7 + c] * (1 / SCALE**2) for c in range(3)]
            found = found + joined(dot_t(thirds(stack(back, 8)), other))
        out_ref[...] += found
        return carry

    lax.fori_loop(0, (total + LANES - 1) // LANES, tile, 0)


def listed(list_ref):
    rows = [list_ref[k : k + 1, :] for k in range(7)]
    return [row if k in (2, 5, 6) else row.astype(I32) for k, row in enumerate(rows)]


def local_kernel(
    poses_in_ref, list_ref, offset_ref, radius_ref,
    out_ref, table_ref,
    poses_ref, u_ref, w_ref, v_ref,
):
    group = lax.axis_index("group")
    blank = jnp.zeros((LANES - KINDS, SUB), F32)
    for e in range(4):
        rows = radius_ref[...] if e == 3 else offset_ref[:, e, :]
        hi = rows.astype(BF16).astype(F32)
        mid = (rows - hi).astype(BF16).astype(F32)
        low = rows - hi - mid
        table_ref[e * SUB : (e + 1) * SUB, :LANES] = jnp.concatenate([hi, mid], 0).T.astype(BF16)
        table_ref[e * SUB : (e + 1) * SUB, LANES:] = jnp.concatenate([low, blank], 0).T.astype(BF16)
    poses_ref[...] = thirds(poses_in_ref[...])
    out_ref[...] = jnp.zeros_like(out_ref)
    first, second, neck, cross_first, cross, cross_neck, export = listed(list_ref)
    ours = (cross >> 5 == group) & (iota((1, LANES), 1) < 64)
    slot = joined(dot(thirds(stack([export], 16)), hot(cross, LANES)))[0:1]
    partner = (first + 1 + second) & (GRAINS_DEV - 1)
    ranks, parts, total = compact(
        [second < GRAINS_DEV - 1, ours],
        [
            [(first + 1).astype(F32), (partner + 1).astype(F32), neck],
            [(cross_first + 1).astype(F32), slot + 1, cross_neck],
        ],
    )
    tiles(total, ranks, parts, poses_ref, poses_ref, table_ref, out_ref, u_ref, w_ref, v_ref, True)


def remote_kernel(
    poses_in_ref, list_ref, table_ref, local_ref, velocity_ref, accel_ref, spin_ref, before_ref, after_ref, far1_ref, far2_ref, far3_ref,
    velocity_out_ref, spin_out_ref,
    poses_ref, pool_ref, out_ref, u_ref, w_ref, v_ref,
):
    group = lax.axis_index("group")
    lane = iota((1, LANES), 1)
    poses_ref[...] = thirds(poses_in_ref[...])
    fars = (far1_ref, far2_ref, far3_ref)
    pool = [before_ref[0:16, :], after_ref[0:16, :], before_ref[16:32, :], after_ref[16:32, :]]
    pool_ref[...] = thirds(jnp.concatenate(pool + [f[...] for f in fars], 1))
    out_ref[...] = local_ref[...]
    actives, fields = [], []

    def add(active, own, place, neck):
        actives.append(active)
        fields.append([(own + 1).astype(F32), (place + 1).astype(F32), neck])

    first, second, neck, cross_first, cross, cross_neck, export = listed(list_ref)
    beyond = second - (GRAINS_DEV - 1)
    add(beyond >= 0, first, beyond, neck)
    way = (group - (cross >> 5)) & 3
    add(
        (way != 0) & (lane < 64),
        cross_first,
        3 * LANES + way * LANES + 64 + (cross & (CX - 1)),
        cross_neck,
    )
    beyond = before_ref[29:30, :].astype(I32) - (GRAINS_DEV - 1)
    add(beyond >= BOUND_DEV, beyond - BOUND_DEV, 2 * LANES + lane, before_ref[30:31, :])
    beyond = after_ref[29:30, :].astype(I32) - (GRAINS_DEV - 1)
    add((beyond >= 0) & (beyond < BOUND_DEV), beyond, 3 * LANES + lane, after_ref[30:31, :])
    exports = thirds(stack([export], 16))
    for k in (1, 2, 3):
        wanted = fars[k - 1][13:14, :].astype(I32)
        sender = (group - k) & 3
        slot = joined(dot(exports, hot(sender * CX + (wanted & (CX - 1)), LANES)))[0:1]
        add(
            (wanted >> 5 == group) & (lane < 64),
            slot,
            (3 + k) * LANES + lane,
            fars[k - 1][14:15, :],
        )
    ranks, parts, total = compact(actives, fields)
    tiles(total, ranks, parts, pool_ref, poses_ref, table_ref, out_ref, u_ref, w_ref, v_ref, False)
    velocity_out_ref[...] = velocity_ref[...] + 0.5 * time_step * (accel_ref[...] + out_ref[0:3, :])
    spin_out_ref[...] = spin_ref[...] + time_step * out_ref[3:6, :] / inertia


def shifted(array, axis, by):
    devices = lax.axis_size(axis)
    return lax.ppermute(array, axis, [(i, (i + by) % devices) for i in range(devices)])


def shape(rows, columns, kind=F32):
    return jax.ShapeDtypeStruct((rows, columns), kind)


def on_device(
    position, velocity, accel_old, orientation, spin, shape_index, shape_offsets, shape_radii,
    pair_first, pair_second, pair_neck, cross_first, cross_second, cross_neck, export_slots,
):
    row = lambda x: x.reshape(1, x.shape[0])
    sources = (position, velocity, accel_old, orientation) + tuple(
        row(x)
        for x in (
            shape_index, pair_first, pair_second, pair_neck, cross_first, cross_second, cross_neck, export_slots
        )
    )
    moved, poses, lists, near, far1, far2, far3 = pl.pallas_call(
        prepare_kernel,
        in_specs=[pl.BlockSpec(memory_space=pltpu.MemorySpace.HBM)] * 12,
        out_shape=(
            shape(3, GRAINS_DEV), shape(16, GRAINS_DEV), shape(8, LANES), shape(32, LANES),
            shape(16, LANES), shape(16, LANES), shape(16, LANES),
        ),
        scratch_shapes=[pltpu.VMEM(x.shape, x.dtype) for x in sources] + [pltpu.SemaphoreType.DMA((12,))],
        compiler_params=pltpu.CompilerParams(vmem_limit_bytes=60 << 20),
        name="prepare",
    )(*sources)
    before = shifted(near, "region", 1)
    after = shifted(near, "region", -1)
    fars = [shifted(f, "group", k) for k, f in ((1, far1), (2, far2), (3, far3))]
    work = [
        pltpu.VMEM((4, PARTS, SUB, LANES), F32),
        pltpu.VMEM((4, PARTS, SUB, LANES), F32),
        pltpu.VMEM((4, SUB, LANES), F32),
    ]
    local, table = pl.pallas_call(
        local_kernel,
        out_shape=(shape(8, GRAINS_DEV), shape(4 * SUB, 4 * KINDS, BF16)),
        scratch_shapes=[pltpu.VMEM((48, GRAINS_DEV), BF16)] + work,
        compiler_params=pltpu.CompilerParams(vmem_limit_bytes=32 << 20),
        cost_estimate=pl.CostEstimate(flops=4_000_000_000, bytes_accessed=1_000_000, transcendentals=4_000_000),
        name="local",
    )(poses, lists, shape_offsets, shape_radii)
    velocity_new, spin_new = pl.pallas_call(
        remote_kernel,
        out_shape=(shape(3, GRAINS_DEV), shape(3, GRAINS_DEV)),
        scratch_shapes=[
            pltpu.VMEM((48, GRAINS_DEV), BF16), pltpu.VMEM((48, 7 * LANES), BF16), pltpu.VMEM((8, GRAINS_DEV), F32)
        ] + work,
        compiler_params=pltpu.CompilerParams(vmem_limit_bytes=32 << 20),
        name="remote",
    )(poses, lists, table, local, velocity, accel_old, spin, before, after, *fars)
    return (moved, velocity_new, spin_new)


def solution(mesh):
    both = ("group", "region")
    wide_spec, flat = P(None, both), P(both)
    return jax.shard_map(
        on_device,
        mesh=mesh,
        in_specs=(wide_spec,) * 5 + (flat, P(), P()) + (flat,) * 7,
        out_specs=(wide_spec,) * 3,
        check_vma=False,
    )
```

```python
import functools
import math

import jax
import jax.numpy as jnp
from jax import lax
from jax.experimental import pallas as pl
from jax.experimental.pallas import tpu as pltpu
from jax.sharding import PartitionSpec as P

F32 = jnp.float32
BF16 = jnp.bfloat16
I32 = jnp.int32

BOUND_DEV = 128
CX = 32
KINDS = 64
SUB = 128
GRAINS_DEV = 1024
LANES = 128
HALVES = 2
WIDTH = HALVES * LANES

time_step = 0.05
stiffness = 0.0078125
cohesion = 0.05
inertia = 0.4

SCALE = math.sqrt(math.log2(math.e) / 4)
SOFT = 0.01 * SCALE * SCALE
LIFT = 2.0**SOFT
GAIN = LIFT * SCALE * stiffness
BOND = LIFT * SCALE * cohesion
DRAG = LIFT * stiffness


def iota(shape, dim):
    return lax.broadcasted_iota(I32, shape, dim)


def thirds(x):
    hi = x.astype(BF16).astype(F32)
    rest = x - hi
    mid = rest.astype(BF16).astype(F32)
    return jnp.concatenate([hi, mid, rest - mid], 0).astype(BF16)


def joined(y):
    n = y.shape[0] // 3
    return (y[2 * n :] + y[n : 2 * n]) + y[:n]


def dot(a, b):
    return lax.dot_general(a, b, (((1,), (0,)), ((), ())), preferred_element_type=F32)


def dot_t(a, b):
    return lax.dot_general(a, b, (((1,), (1,)), ((), ())), preferred_element_type=F32)


def hot(index, count):
    return jnp.where(iota((count, index.shape[1]), 0) == index, 1.0, 0.0).astype(BF16)


def wide(row):
    return jnp.concatenate([row, jnp.zeros((1, LANES - row.shape[1]), row.dtype)], 1)


def stack(rows, count):
    at = iota((count, rows[0].shape[1]), 0)
    out = jnp.zeros((count, rows[0].shape[1]), F32)
    for k, row in enumerate(rows):
        out = jnp.where(at == k, row, out)
    return out


def compact(actives, fields):
    segments = len(actives)
    flags = stack([a.astype(F32) for a in actives], 16)
    below = jnp.where(iota((LANES, LANES), 0) < iota((LANES, LANES), 1), 1.0, 0.0).astype(BF16)
    inside = dot(flags.astype(BF16), below)
    sums = dot(flags.astype(BF16), jnp.ones((LANES, LANES), BF16))
    ranks = []
    before = jnp.zeros((1, LANES), F32)
    for s in range(segments):
        ranks.append(jnp.where(actives[s], inside[s : s + 1] + before, -1.0).astype(I32))
        before = before + sums[s : s + 1]
    total = jnp.sum(flags).astype(I32)
    parts = thirds(jnp.concatenate([stack(f, 16) for f in fields], 1))
    return jnp.concatenate(ranks, 1), parts, total


def picked(ranks, parts, base):
    want = iota((WIDTH, ranks.shape[1]), 0) + base
    chosen = jnp.where(want == ranks, 1.0, 0.0).astype(BF16)
    return joined(dot_t(parts, chosen))


def worlds(table_ref, pose):
    at = iota((4 * KINDS, pose.shape[1]), 0)
    kinds = jnp.where(((at & (KINDS - 1)) == pose[12:13].astype(I32)) & (at < 3 * KINDS), 1.0, 0.0).astype(BF16)
    shapes = dot(table_ref[...], kinds)
    offset = [shapes[e * SUB : (e + 1) * SUB] for e in range(4)]
    turn = [SCALE * pose[3 + n : 4 + n] for n in range(9)]
    return [
        turn[3 * c] * offset[0] + turn[3 * c + 1] * offset[1] + turn[3 * c + 2] * offset[2] for c in range(3)
    ] + [GAIN * offset[3]]


def interact(u, v_ref):
    def step(b, sums):
        v = [v_ref[c, pl.ds(b, 8, stride=0), :] for c in range(4)]
        out = []
        for one, s in zip(u, sums):
            x, y, z = (one[c] - v[c] for c in range(3))
            square = (x * x + SOFT) + y * y + z * z
            m = ((one[3] + v[3]) * lax.rsqrt(square) - DRAG) * jnp.exp2(-square)
            out.append((s[0] + m * x, s[1] + m * y, s[2] + m * z))
        return tuple(out)

    zero = jnp.zeros((8, LANES), F32)
    sums = lax.fori_loop(0, SUB, step, ((zero,) * 3,) * len(u), unroll=16)
    rows = [zero] * 6
    for one, g in zip(u, sums):
        for c in range(3):
            n, o = (c + 1) % 3, (c + 2) % 3
            rows[c] = rows[c] + g[c]
            rows[3 + c] = rows[3 + c] + (one[n] * g[o] - one[o] * g[n])
    return stack([jnp.sum(t, 0, keepdims=True) for t in rows], 8)


def full_tile(u_ref, w_ref):
    rows = SUB // 4

    def quarter(h, terms):
        u = [[u_ref[c, pl.ds(h * rows + 8 * k, 8), :] for c in range(4)] for k in range(rows // 8)]
        return terms + interact(u, w_ref)

    return lax.fori_loop(0, 4, quarter, jnp.zeros((8, LANES), F32))


def unit(start, width, u_ref, w_ref, v_ref):
    parts = LANES // width
    rows = SUB // parts
    def wanted(count):
        lane = iota((count, LANES), 1)
        return (lane >= start) & (lane < start + width)

    def copied(block):
        block = jnp.where(wanted(SUB), block, 0.0)
        step = width
        while step < LANES:
            block = block + pltpu.roll(block, step, 1)
            step *= 2
        return block

    def dealt(blocks):
        out = jnp.where(wanted(rows), blocks[0], 0.0)
        for h in range(1, parts):
            out = out + pltpu.roll(jnp.where(wanted(rows), blocks[h], 0.0), h * width, 1)
        return pltpu.roll(out, (LANES - start) & (LANES - 1), 1)

    for c in range(4):
        v_ref[c] = copied(w_ref[c])
    mine = [dealt([u_ref[c, h * rows : (h + 1) * rows, :] for h in range(parts)]) for c in range(4)]
    u = [[mine[c][8 * k : 8 * k + 8] for c in range(4)] for k in range(rows // 8)]
    found = interact(u, v_ref)
    step = LANES // 2
    while step >= width:
        found = found + pltpu.roll(found, step, 1)
        step //= 2
    return jnp.where(wanted(8), found, 0.0)


def part_tile(count, u_ref, w_ref, v_ref):
    whole = (count + 15) // 32

    def step(n, terms):
        return terms + unit(n * 32, 32, u_ref, w_ref, v_ref)

    terms = lax.fori_loop(0, whole, step, jnp.zeros((8, LANES), F32))
    return lax.cond(
        count > whole * 32, lambda: terms + unit(whole * 32, 16, u_ref, w_ref, v_ref), lambda: terms
    )


def prepare_kernel(
    position_hbm, velocity_hbm, accel_hbm, turn_hbm, kind_hbm, first_hbm, second_hbm, neck_hbm,
    cross_first_hbm, cross_second_hbm, cross_neck_hbm, export_hbm,
    moved_ref, pose_ref, list_ref, near_ref, far1_ref, far2_ref, far3_ref,
    position_ref, velocity_ref, accel_ref, turn_ref, kind_ref, first_ref, second_ref, neck_ref,
    cross_first_ref, cross_second_ref, cross_neck_ref, export_ref, sems,
):
    sources = (
        position_hbm, velocity_hbm, accel_hbm, turn_hbm, kind_hbm, first_hbm, second_hbm, neck_hbm,
        cross_first_hbm, cross_second_hbm, cross_neck_hbm, export_hbm,
    )
    targets = (
        position_ref, velocity_ref, accel_ref, turn_ref, kind_ref, first_ref, second_ref, neck_ref,
        cross_first_ref, cross_second_ref, cross_neck_ref, export_ref,
    )
    copies = [pltpu.make_async_copy(a, b, sems.at[k]) for k, (a, b) in enumerate(zip(sources, targets))]
    for copy in copies:
        copy.start()
    for copy in copies:
        copy.wait()
    group = lax.axis_index("group")
    moved = position_ref[...] + time_step * velocity_ref[...] + 0.5 * time_step**2 * accel_ref[...]
    moved_ref[...] = moved
    pose_ref[0:3, :] = moved
    pose_ref[3:12, :] = turn_ref[...]
    pose_ref[12:13, :] = kind_ref[...].astype(F32)
    pose_ref[13:16, :] = jnp.zeros((3, GRAINS_DEV), F32)
    index = jnp.concatenate([first_ref[...], wide(cross_first_ref[...]), export_ref[...]], 1)
    got = joined(dot(thirds(pose_ref[...]), hot(index, GRAINS_DEV)))
    at = iota((16, LANES), 0)
    second, neck = second_ref[...].astype(F32), neck_ref[...]
    cross_second, cross_neck = wide(cross_second_ref[...]).astype(F32), wide(cross_neck_ref[...])
    near_ref[0:16, :] = pose_ref[:, :BOUND_DEV]
    near_ref[16:32, :] = jnp.where(at == 14, neck, jnp.where(at == 13, second, got[:, :LANES]))
    listed = jnp.where(at == 14, cross_neck, jnp.where(at == 13, cross_second, got[:, LANES : 2 * LANES]))
    exported = got[:, 2 * LANES :]
    for k, far_ref in ((1, far1_ref), (2, far2_ref), (3, far3_ref)):
        to = (group + k) & 3
        turned = pltpu.roll(exported, (64 - CX * to) & (LANES - 1), 1)
        far_ref[...] = jnp.where(iota((16, LANES), 1) < 64, listed, turned)
    first, cross_first = first_ref[...].astype(F32), wide(cross_first_ref[...]).astype(F32)
    list_ref[...] = stack(
        [first, second, neck, cross_first, cross_second, cross_neck, export_ref[...].astype(F32)], 8
    )


def tiles(total, ranks, parts, other_of, poses_ref, table_ref, out_ref, work, both):
    u_ref, w_ref, v_ref, terms_ref = work

    def tile(t, carry):
        fields = picked(ranks, parts, t * WIDTH)
        own = hot(fields[0:1].astype(I32) - 1, GRAINS_DEV)
        mine = joined(dot(poses_ref[...], own))
        other = hot(fields[1:2].astype(I32) - 1, other_of.shape[1])
        theirs = joined(dot(other_of[...], other))
        shift = [SCALE * (mine[c : c + 1] - theirs[c : c + 1]) for c in range(3)]
        second = worlds(table_ref, theirs)
        first = worlds(table_ref, mine)
        first = [first[c] + shift[c] for c in range(3)] + [first[3] - BOND * fields[2:3]]
        for n in range(HALVES):
            for c in range(4):
                w_ref[n, c] = second[c][:, n * LANES : (n + 1) * LANES]
                u_ref[n, c] = first[c][:, n * LANES : (n + 1) * LANES]
        terms_ref[...] = jnp.zeros_like(terms_ref)
        left = total - t * WIDTH

        def half(n, none):
            count = jnp.minimum(left - n * LANES, LANES)
            terms_ref[n] = lax.cond(
                count > 96,
                lambda: full_tile(u_ref.at[n], w_ref.at[n]),
                lambda: part_tile(count, u_ref.at[n], w_ref.at[n], v_ref),
            )
            return none

        lax.fori_loop(0, jnp.minimum(HALVES, (left + LANES - 1) // LANES), half, 0)
        terms = jnp.concatenate([terms_ref[n] for n in range(HALVES)], 1)
        force = [terms[c : c + 1] for c in range(3)]
        rows = [f * (1 / SCALE) for f in force]
        for c in range(3):
            n, o = (c + 1) % 3, (c + 2) % 3
            rows.append((terms[3 + c : 4 + c] - (shift[n] * force[o] - shift[o] * force[n])) * (1 / SCALE**2))
        found = joined(dot_t(thirds(stack(rows, 8)), own))
        if both:
            back = [-r for r in rows[:3]] + [terms[3 + c : 4 + c] * (-1 / SCALE**2) for c in range(3)]
            found = found + joined(dot_t(thirds(stack(back, 8)), other))
        out_ref[...] += found
        return carry

    lax.fori_loop(0, (total + WIDTH - 1) // WIDTH, tile, 0)


def listed(list_ref):
    rows = [list_ref[k : k + 1, :] for k in range(7)]
    return [row if k in (2, 5, 6) else row.astype(I32) for k, row in enumerate(rows)]


def local_kernel(
    poses_in_ref, list_ref, offset_ref, radius_ref,
    out_ref, table_ref,
    poses_ref, *work,
):
    group = lax.axis_index("group")
    blank = jnp.zeros((LANES - KINDS, SUB), F32)
    for e in range(4):
        rows = radius_ref[...] if e == 3 else offset_ref[:, e, :]
        hi = rows.astype(BF16).astype(F32)
        mid = (rows - hi).astype(BF16).astype(F32)
        low = rows - hi - mid
        table_ref[e * SUB : (e + 1) * SUB, :LANES] = jnp.concatenate([hi, mid], 0).T.astype(BF16)
        table_ref[e * SUB : (e + 1) * SUB, LANES:] = jnp.concatenate([low, blank], 0).T.astype(BF16)
    poses_ref[...] = thirds(poses_in_ref[...])
    out_ref[...] = jnp.zeros_like(out_ref)
    first, second, neck, cross_first, cross, cross_neck, export = listed(list_ref)
    ours = (cross >> 5 == group) & (iota((1, LANES), 1) < 64)
    slot = joined(dot(thirds(stack([export], 16)), hot(cross, LANES)))[0:1]
    partner = (first + 1 + second) & (GRAINS_DEV - 1)
    ranks, parts, total = compact(
        [second < GRAINS_DEV - 1, ours],
        [
            [(first + 1).astype(F32), (partner + 1).astype(F32), neck],
            [(cross_first + 1).astype(F32), slot + 1, cross_neck],
        ],
    )
    tiles(total, ranks, parts, poses_ref, poses_ref, table_ref, out_ref, work, True)


def remote_kernel(
    poses_in_ref, list_ref, table_ref, local_ref, velocity_ref, accel_ref, spin_ref, before_ref, after_ref, far1_ref, far2_ref, far3_ref,
    velocity_out_ref, spin_out_ref,
    poses_ref, pool_ref, out_ref, *work,
):
    group = lax.axis_index("group")
    lane = iota((1, LANES), 1)
    poses_ref[...] = thirds(poses_in_ref[...])
    fars = (far1_ref, far2_ref, far3_ref)
    pool = [before_ref[0:16, :], after_ref[0:16, :], before_ref[16:32, :], after_ref[16:32, :]]
    pool_ref[...] = thirds(jnp.concatenate(pool + [f[...] for f in fars], 1))
    out_ref[...] = local_ref[...]
    actives, fields = [], []

    def add(active, own, place, neck):
        actives.append(active)
        fields.append([(own + 1).astype(F32), (place + 1).astype(F32), neck])

    first, second, neck, cross_first, cross, cross_neck, export = listed(list_ref)
    beyond = second - (GRAINS_DEV - 1)
    add(beyond >= 0, first, beyond, neck)
    way = (group - (cross >> 5)) & 3
    add(
        (way != 0) & (lane < 64),
        cross_first,
        3 * LANES + way * LANES + 64 + (cross & (CX - 1)),
        cross_neck,
    )
    beyond = before_ref[29:30, :].astype(I32) - (GRAINS_DEV - 1)
    add(beyond >= BOUND_DEV, beyond - BOUND_DEV, 2 * LANES + lane, before_ref[30:31, :])
    beyond = after_ref[29:30, :].astype(I32) - (GRAINS_DEV - 1)
    add((beyond >= 0) & (beyond < BOUND_DEV), beyond, 3 * LANES + lane, after_ref[30:31, :])
    exports = thirds(stack([export], 16))
    for k in (1, 2, 3):
        wanted = fars[k - 1][13:14, :].astype(I32)
        sender = (group - k) & 3
        slot = joined(dot(exports, hot(sender * CX + (wanted & (CX - 1)), LANES)))[0:1]
        add(
            (wanted >> 5 == group) & (lane < 64),
            slot,
            (3 + k) * LANES + lane,
            fars[k - 1][14:15, :],
        )
    ranks, parts, total = compact(actives, fields)
    tiles(total, ranks, parts, pool_ref, poses_ref, table_ref, out_ref, work, False)
    velocity_out_ref[...] = velocity_ref[...] + 0.5 * time_step * (accel_ref[...] + out_ref[0:3, :])
    spin_out_ref[...] = spin_ref[...] + time_step * out_ref[3:6, :] / inertia


def shifted(array, axis, by):
    devices = lax.axis_size(axis)
    return lax.ppermute(array, axis, [(i, (i + by) % devices) for i in range(devices)])


def shape(rows, columns, kind=F32):
    return jax.ShapeDtypeStruct((rows, columns), kind)


def on_device(
    position, velocity, accel_old, orientation, spin, shape_index, shape_offsets, shape_radii,
    pair_first, pair_second, pair_neck, cross_first, cross_second, cross_neck, export_slots,
):
    row = lambda x: x.reshape(1, x.shape[0])
    sources = (position, velocity, accel_old, orientation) + tuple(
        row(x)
        for x in (
            shape_index, pair_first, pair_second, pair_neck, cross_first, cross_second, cross_neck, export_slots
        )
    )
    moved, poses, lists, near, far1, far2, far3 = pl.pallas_call(
        prepare_kernel,
        in_specs=[pl.BlockSpec(memory_space=pltpu.MemorySpace.HBM)] * 12,
        out_shape=(
            shape(3, GRAINS_DEV), shape(16, GRAINS_DEV), shape(8, LANES), shape(32, LANES),
            shape(16, LANES), shape(16, LANES), shape(16, LANES),
        ),
        scratch_shapes=[pltpu.VMEM(x.shape, x.dtype) for x in sources] + [pltpu.SemaphoreType.DMA((12,))],
        compiler_params=pltpu.CompilerParams(vmem_limit_bytes=60 << 20),
        name="prepare",
    )(*sources)
    before = shifted(near, "region", 1)
    after = shifted(near, "region", -1)
    fars = [shifted(f, "group", k) for k, f in ((1, far1), (2, far2), (3, far3))]
    work = [
        pltpu.VMEM((HALVES, 4, SUB, LANES), F32),
        pltpu.VMEM((HALVES, 4, SUB, LANES), F32),
        pltpu.VMEM((4, SUB, LANES), F32),
        pltpu.VMEM((HALVES, 8, LANES), F32),
    ]
    local, table = pl.pallas_call(
        local_kernel,
        out_shape=(shape(8, GRAINS_DEV), shape(4 * SUB, 4 * KINDS, BF16)),
        scratch_shapes=[pltpu.VMEM((48, GRAINS_DEV), BF16)] + work,
        compiler_params=pltpu.CompilerParams(vmem_limit_bytes=32 << 20),
        cost_estimate=pl.CostEstimate(flops=4_000_000_000, bytes_accessed=1_000_000, transcendentals=4_000_000),
        name="local",
    )(poses, lists, shape_offsets, shape_radii)
    velocity_new, spin_new = pl.pallas_call(
        remote_kernel,
        out_shape=(shape(3, GRAINS_DEV), shape(3, GRAINS_DEV)),
        scratch_shapes=[
            pltpu.VMEM((48, GRAINS_DEV), BF16), pltpu.VMEM((48, 7 * LANES), BF16), pltpu.VMEM((8, GRAINS_DEV), F32)
        ] + work,
        compiler_params=pltpu.CompilerParams(vmem_limit_bytes=32 << 20),
        name="remote",
    )(poses, lists, table, local, velocity, accel_old, spin, before, after, *fars)
    return (moved, velocity_new, spin_new)


def solution(mesh):
    both = ("group", "region")
    wide_spec, flat = P(None, both), P(both)
    return jax.shard_map(
        on_device,
        mesh=mesh,
        in_specs=(wide_spec,) * 5 + (flat, P(), P()) + (flat,) * 7,
        out_specs=(wide_spec,) * 3,
        check_vma=False,
    )
```

```python
import functools
import math

import jax
import jax.numpy as jnp
from jax import lax
from jax.experimental import pallas as pl
from jax.experimental.pallas import tpu as pltpu
from jax.sharding import PartitionSpec as P

F32 = jnp.float32
BF16 = jnp.bfloat16
I32 = jnp.int32

BOUND_DEV = 128
CX = 32
KINDS = 64
SUB = 128
GRAINS_DEV = 1024
LANES = 128
HALVES = 2
WIDTH = HALVES * LANES

time_step = 0.05
stiffness = 0.0078125
cohesion = 0.05
inertia = 0.4

SCALE = math.sqrt(math.log2(math.e) / 4)
SOFT = 0.01 * SCALE * SCALE
LIFT = 2.0**SOFT
GAIN = LIFT * SCALE * stiffness
BOND = LIFT * SCALE * cohesion
DRAG = LIFT * stiffness


def iota(shape, dim):
    return lax.broadcasted_iota(I32, shape, dim)


def thirds(x):
    hi = x.astype(BF16).astype(F32)
    rest = x - hi
    mid = rest.astype(BF16).astype(F32)
    return jnp.concatenate([hi, mid, rest - mid], 0).astype(BF16)


def joined(y):
    n = y.shape[0] // 3
    return (y[2 * n :] + y[n : 2 * n]) + y[:n]


def dot(a, b):
    return lax.dot_general(a, b, (((1,), (0,)), ((), ())), preferred_element_type=F32)


def dot_t(a, b):
    return lax.dot_general(a, b, (((1,), (1,)), ((), ())), preferred_element_type=F32)


def hot(index, count):
    return jnp.where(iota((count, index.shape[1]), 0) == index, 1.0, 0.0).astype(BF16)


def wide(row):
    return jnp.concatenate([row, jnp.zeros((1, LANES - row.shape[1]), row.dtype)], 1)


def stack(rows, count):
    at = iota((count, rows[0].shape[1]), 0)
    out = jnp.zeros((count, rows[0].shape[1]), F32)
    for k, row in enumerate(rows):
        out = jnp.where(at == k, row, out)
    return out


def compact(actives, fields):
    segments = len(actives)
    flags = stack([a.astype(F32) for a in actives], 16)
    below = jnp.where(iota((LANES, LANES), 0) < iota((LANES, LANES), 1), 1.0, 0.0).astype(BF16)
    inside = dot(flags.astype(BF16), below)
    sums = dot(flags.astype(BF16), jnp.ones((LANES, LANES), BF16))
    ranks = []
    before = jnp.zeros((1, LANES), F32)
    for s in range(segments):
        ranks.append(jnp.where(actives[s], inside[s : s + 1] + before, -1.0).astype(I32))
        before = before + sums[s : s + 1]
    total = jnp.sum(flags).astype(I32)
    parts = thirds(jnp.concatenate([stack(f, 16) for f in fields], 1))
    return jnp.concatenate(ranks, 1), parts, total


def picked(ranks, parts, base, widths):
    at = iota((WIDTH, ranks.shape[1]), 0)
    want = base + jnp.where(at < LANES, at & (widths[0] - 1), LANES + (at & (widths[1] - 1)))
    chosen = jnp.where(want == ranks, 1.0, 0.0).astype(BF16)
    return joined(dot_t(parts, chosen))


def worlds(table_ref, pose):
    at = iota((4 * KINDS, pose.shape[1]), 0)
    kinds = jnp.where(((at & (KINDS - 1)) == pose[12:13].astype(I32)) & (at < 3 * KINDS), 1.0, 0.0).astype(BF16)
    shapes = dot(table_ref[...], kinds)
    offset = [shapes[e * SUB : (e + 1) * SUB] for e in range(4)]
    turn = [SCALE * pose[3 + n : 4 + n] for n in range(9)]
    return [
        turn[3 * c] * offset[0] + turn[3 * c + 1] * offset[1] + turn[3 * c + 2] * offset[2] for c in range(3)
    ] + [GAIN * offset[3]]


def interact(u, v_ref):
    def step(b, sums):
        v = [v_ref[c, pl.ds(b, 8, stride=0), :] for c in range(4)]
        out = []
        for one, s in zip(u, sums):
            x, y, z = (one[c] - v[c] for c in range(3))
            square = (x * x + SOFT) + y * y + z * z
            m = ((one[3] + v[3]) * lax.rsqrt(square) - DRAG) * jnp.exp2(-square)
            out.append((s[0] + m * x, s[1] + m * y, s[2] + m * z))
        return tuple(out)

    zero = jnp.zeros((8, LANES), F32)
    sums = lax.fori_loop(0, SUB, step, ((zero,) * 3,) * len(u), unroll=16)
    rows = [zero] * 6
    for one, g in zip(u, sums):
        for c in range(3):
            n, o = (c + 1) % 3, (c + 2) % 3
            rows[c] = rows[c] + g[c]
            rows[3 + c] = rows[3 + c] + (one[n] * g[o] - one[o] * g[n])
    return rows


def dealt(u_ref, width):
    rows = SUB * width // LANES
    part = iota((rows, LANES), 1) // width
    for c in range(4):
        value = u_ref[c, :rows, :]
        for h in range(1, LANES // width):
            value = jnp.where(part == h, u_ref[c, h * rows : (h + 1) * rows, :], value)
        u_ref[c, :rows, :] = value


def half_tile(width, u_ref, w_ref):
    def blocks(h, count):
        return [[u_ref[c, pl.ds(h * 32 + 8 * k, 8), :] for c in range(4)] for k in range(count)]

    for size in (64, 32, 16):
        pl.when(width == size)(functools.partial(dealt, u_ref, size))
    zero = (jnp.zeros((8, LANES), F32),) * 6

    def whole():
        def step(h, terms):
            return tuple(a + b for a, b in zip(terms, interact(blocks(h, 4), w_ref)))

        return lax.fori_loop(0, width // 32, step, zero)

    terms = lax.cond(width == 16, lambda: tuple(interact(blocks(0, 2), w_ref)), whole)
    return stack([jnp.sum(t, 0, keepdims=True) for t in terms], 8)


def prepare_kernel(
    position_hbm, velocity_hbm, accel_hbm, turn_hbm, kind_hbm, first_hbm, second_hbm, neck_hbm,
    cross_first_hbm, cross_second_hbm, cross_neck_hbm, export_hbm,
    moved_ref, thirds_ref, list_ref, near_ref, far1_ref, far2_ref, far3_ref,
    position_ref, velocity_ref, accel_ref, turn_ref, kind_ref, first_ref, second_ref, neck_ref,
    cross_first_ref, cross_second_ref, cross_neck_ref, export_ref, pose_ref, sems,
):
    sources = (
        position_hbm, velocity_hbm, accel_hbm, turn_hbm, kind_hbm, first_hbm, second_hbm, neck_hbm,
        cross_first_hbm, cross_second_hbm, cross_neck_hbm, export_hbm,
    )
    targets = (
        position_ref, velocity_ref, accel_ref, turn_ref, kind_ref, first_ref, second_ref, neck_ref,
        cross_first_ref, cross_second_ref, cross_neck_ref, export_ref,
    )
    copies = [pltpu.make_async_copy(a, b, sems.at[k]) for k, (a, b) in enumerate(zip(sources, targets))]
    for copy in copies:
        copy.start()
    for copy in copies:
        copy.wait()
    group = lax.axis_index("group")
    moved = position_ref[...] + time_step * velocity_ref[...] + 0.5 * time_step**2 * accel_ref[...]
    moved_ref[...] = moved
    pose_ref[0:3, :] = moved
    pose_ref[3:12, :] = turn_ref[...]
    pose_ref[12:13, :] = kind_ref[...].astype(F32)
    pose_ref[13:16, :] = jnp.zeros((3, GRAINS_DEV), F32)
    index = jnp.concatenate([first_ref[...], wide(cross_first_ref[...]), export_ref[...]], 1)
    poses = thirds(pose_ref[...])
    thirds_ref[...] = poses
    got = joined(dot(poses, hot(index, GRAINS_DEV)))
    at = iota((16, LANES), 0)
    second, neck = second_ref[...].astype(F32), neck_ref[...]
    cross_second, cross_neck = wide(cross_second_ref[...]).astype(F32), wide(cross_neck_ref[...])
    near_ref[0:16, :] = pose_ref[:, :BOUND_DEV]
    near_ref[16:32, :] = jnp.where(at == 14, neck, jnp.where(at == 13, second, got[:, :LANES]))
    listed = jnp.where(at == 14, cross_neck, jnp.where(at == 13, cross_second, got[:, LANES : 2 * LANES]))
    exported = got[:, 2 * LANES :]
    for k, far_ref in ((1, far1_ref), (2, far2_ref), (3, far3_ref)):
        to = (group + k) & 3
        turned = pltpu.roll(exported, (64 - CX * to) & (LANES - 1), 1)
        far_ref[...] = jnp.where(iota((16, LANES), 1) < 64, listed, turned)
    first, cross_first = first_ref[...].astype(F32), wide(cross_first_ref[...]).astype(F32)
    list_ref[...] = stack(
        [first, second, neck, cross_first, cross_second, cross_neck, export_ref[...].astype(F32)], 8
    )


def tiles(total, ranks, parts, other_of, poses_ref, table_ref, out_ref, work, both):
    u_ref, w_ref, terms_ref = work

    def tile(t, carry):
        left = total - t * WIDTH
        counts = [left - n * LANES for n in range(HALVES)]
        widths = [
            jnp.where(n <= 16, 16, jnp.where(n <= 32, 32, jnp.where(n <= 64, 64, LANES))).astype(I32) for n in counts
        ]
        fields = picked(ranks, parts, t * WIDTH, widths)
        own = hot(fields[0:1].astype(I32) - 1, GRAINS_DEV)
        mine = joined(dot(poses_ref[...], own))
        other = hot(fields[1:2].astype(I32) - 1, other_of.shape[1])
        theirs = joined(dot(other_of[...], other))
        shift = [SCALE * (mine[c : c + 1] - theirs[c : c + 1]) for c in range(3)]
        second = worlds(table_ref, theirs)
        first = worlds(table_ref, mine)
        first = [first[c] + shift[c] for c in range(3)] + [first[3] - BOND * fields[2:3]]
        for n in range(HALVES):
            for c in range(4):
                w_ref[n, c] = second[c][:, n * LANES : (n + 1) * LANES]
                u_ref[n, c] = first[c][:, n * LANES : (n + 1) * LANES]
        terms_ref[...] = jnp.zeros_like(terms_ref)

        def half(n, none):
            width = jnp.where(n == 0, widths[0], widths[1])
            terms_ref[n] = half_tile(width, u_ref.at[n], w_ref.at[n])
            return none

        lax.fori_loop(0, jnp.minimum(HALVES, (left + LANES - 1) // LANES), half, 0)
        terms = jnp.concatenate([terms_ref[n] for n in range(HALVES)], 1)
        force = [terms[c : c + 1] for c in range(3)]
        rows = [f * (1 / SCALE) for f in force]
        for c in range(3):
            n, o = (c + 1) % 3, (c + 2) % 3
            rows.append((terms[3 + c : 4 + c] - (shift[n] * force[o] - shift[o] * force[n])) * (1 / SCALE**2))
        found = joined(dot_t(thirds(stack(rows, 8)), own))
        if both:
            back = [-r for r in rows[:3]] + [terms[3 + c : 4 + c] * (-1 / SCALE**2) for c in range(3)]
            found = found + joined(dot_t(thirds(stack(back, 8)), other))
        out_ref[...] += found
        return carry

    lax.fori_loop(0, (total + WIDTH - 1) // WIDTH, tile, 0)


def listed(list_ref):
    rows = [list_ref[k : k + 1, :] for k in range(7)]
    return [row if k in (2, 5, 6) else row.astype(I32) for k, row in enumerate(rows)]


def local_kernel(
    poses_ref, list_ref, offset_ref, radius_ref,
    out_ref, table_ref,
    *work,
):
    group = lax.axis_index("group")
    blank = jnp.zeros((LANES - KINDS, SUB), F32)
    for e in range(4):
        rows = radius_ref[...] if e == 3 else offset_ref[:, e, :]
        hi = rows.astype(BF16).astype(F32)
        mid = (rows - hi).astype(BF16).astype(F32)
        low = rows - hi - mid
        table_ref[e * SUB : (e + 1) * SUB, :LANES] = jnp.concatenate([hi, mid], 0).T.astype(BF16)
        table_ref[e * SUB : (e + 1) * SUB, LANES:] = jnp.concatenate([low, blank], 0).T.astype(BF16)
    out_ref[...] = jnp.zeros_like(out_ref)
    first, second, neck, cross_first, cross, cross_neck, export = listed(list_ref)
    ours = (cross >> 5 == group) & (iota((1, LANES), 1) < 64)
    slot = joined(dot(thirds(stack([export], 16)), hot(cross, LANES)))[0:1]
    partner = (first + 1 + second) & (GRAINS_DEV - 1)
    ranks, parts, total = compact(
        [second < GRAINS_DEV - 1, ours],
        [
            [(first + 1).astype(F32), (partner + 1).astype(F32), neck],
            [(cross_first + 1).astype(F32), slot + 1, cross_neck],
        ],
    )
    tiles(total, ranks, parts, poses_ref, poses_ref, table_ref, out_ref, work, True)


def remote_kernel(
    poses_ref, list_ref, table_ref, local_ref, velocity_ref, accel_ref, spin_ref, before_ref, after_ref, far1_ref, far2_ref, far3_ref,
    velocity_out_ref, spin_out_ref,
    pool_ref, out_ref, *work,
):
    group = lax.axis_index("group")
    lane = iota((1, LANES), 1)
    fars = (far1_ref, far2_ref, far3_ref)
    pool = [before_ref[0:16, :], after_ref[0:16, :], before_ref[16:32, :], after_ref[16:32, :]]
    pool_ref[...] = thirds(jnp.concatenate(pool + [f[...] for f in fars], 1))
    out_ref[...] = local_ref[...]
    actives, fields = [], []

    def add(active, own, place, neck):
        actives.append(active)
        fields.append([(own + 1).astype(F32), (place + 1).astype(F32), neck])

    first, second, neck, cross_first, cross, cross_neck, export = listed(list_ref)
    beyond = second - (GRAINS_DEV - 1)
    add(beyond >= 0, first, beyond, neck)
    way = (group - (cross >> 5)) & 3
    add(
        (way != 0) & (lane < 64),
        cross_first,
        3 * LANES + way * LANES + 64 + (cross & (CX - 1)),
        cross_neck,
    )
    beyond = before_ref[29:30, :].astype(I32) - (GRAINS_DEV - 1)
    add(beyond >= BOUND_DEV, beyond - BOUND_DEV, 2 * LANES + lane, before_ref[30:31, :])
    beyond = after_ref[29:30, :].astype(I32) - (GRAINS_DEV - 1)
    add((beyond >= 0) & (beyond < BOUND_DEV), beyond, 3 * LANES + lane, after_ref[30:31, :])
    exports = thirds(stack([export], 16))
    for k in (1, 2, 3):
        wanted = fars[k - 1][13:14, :].astype(I32)
        sender = (group - k) & 3
        slot = joined(dot(exports, hot(sender * CX + (wanted & (CX - 1)), LANES)))[0:1]
        add(
            (wanted >> 5 == group) & (lane < 64),
            slot,
            (3 + k) * LANES + lane,
            fars[k - 1][14:15, :],
        )
    ranks, parts, total = compact(actives, fields)
    tiles(total, ranks, parts, pool_ref, poses_ref, table_ref, out_ref, work, False)
    velocity_out_ref[...] = velocity_ref[...] + 0.5 * time_step * (accel_ref[...] + out_ref[0:3, :])
    spin_out_ref[...] = spin_ref[...] + time_step * out_ref[3:6, :] / inertia


def shifted(array, axis, by):
    devices = lax.axis_size(axis)
    return lax.ppermute(array, axis, [(i, (i + by) % devices) for i in range(devices)])


def shape(rows, columns, kind=F32):
    return jax.ShapeDtypeStruct((rows, columns), kind)


def on_device(
    position, velocity, accel_old, orientation, spin, shape_index, shape_offsets, shape_radii,
    pair_first, pair_second, pair_neck, cross_first, cross_second, cross_neck, export_slots,
):
    row = lambda x: x.reshape(1, x.shape[0])
    sources = (position, velocity, accel_old, orientation) + tuple(
        row(x)
        for x in (
            shape_index, pair_first, pair_second, pair_neck, cross_first, cross_second, cross_neck, export_slots
        )
    )
    moved, poses, lists, near, far1, far2, far3 = pl.pallas_call(
        prepare_kernel,
        in_specs=[pl.BlockSpec(memory_space=pltpu.MemorySpace.HBM)] * 12,
        out_shape=(
            shape(3, GRAINS_DEV), shape(48, GRAINS_DEV, BF16), shape(8, LANES), shape(32, LANES),
            shape(16, LANES), shape(16, LANES), shape(16, LANES),
        ),
        scratch_shapes=[pltpu.VMEM(x.shape, x.dtype) for x in sources]
        + [pltpu.VMEM((16, GRAINS_DEV), F32), pltpu.SemaphoreType.DMA((12,))],
        compiler_params=pltpu.CompilerParams(vmem_limit_bytes=60 << 20),
        name="prepare",
    )(*sources)
    before = shifted(near, "region", 1)
    after = shifted(near, "region", -1)
    fars = [shifted(f, "group", k) for k, f in ((1, far1), (2, far2), (3, far3))]
    work = [
        pltpu.VMEM((HALVES, 4, SUB, LANES), F32),
        pltpu.VMEM((HALVES, 4, SUB, LANES), F32),
        pltpu.VMEM((HALVES, 8, LANES), F32),
    ]
    local, table = pl.pallas_call(
        local_kernel,
        out_shape=(shape(8, GRAINS_DEV), shape(4 * SUB, 4 * KINDS, BF16)),
        scratch_shapes=work,
        compiler_params=pltpu.CompilerParams(vmem_limit_bytes=32 << 20),
        cost_estimate=pl.CostEstimate(flops=4_000_000_000, bytes_accessed=1_000_000, transcendentals=4_000_000),
        name="local",
    )(poses, lists, shape_offsets, shape_radii)
    velocity_new, spin_new = pl.pallas_call(
        remote_kernel,
        out_shape=(shape(3, GRAINS_DEV), shape(3, GRAINS_DEV)),
        scratch_shapes=[
            pltpu.VMEM((48, 7 * LANES), BF16), pltpu.VMEM((8, GRAINS_DEV), F32)
        ] + work,
        compiler_params=pltpu.CompilerParams(vmem_limit_bytes=32 << 20),
        name="remote",
    )(poses, lists, table, local, velocity, accel_old, spin, before, after, *fars)
    return (moved, velocity_new, spin_new)


def solution(mesh):
    both = ("group", "region")
    wide_spec, flat = P(None, both), P(both)
    return jax.shard_map(
        on_device,
        mesh=mesh,
        in_specs=(wide_spec,) * 5 + (flat, P(), P()) + (flat,) * 7,
        out_specs=(wide_spec,) * 3,
        check_vma=False,
    )
```

```python
import functools
import math

import jax
import jax.numpy as jnp
from jax import lax
from jax.experimental import pallas as pl
from jax.experimental.pallas import tpu as pltpu
from jax.sharding import PartitionSpec as P

F32 = jnp.float32
BF16 = jnp.bfloat16
I32 = jnp.int32

BOUND_DEV = 128
CX = 32
KINDS = 64
SUB = 128
GRAINS_DEV = 1024
LANES = 128
HALVES = 2
WIDTH = HALVES * LANES

time_step = 0.05
stiffness = 0.0078125
cohesion = 0.05
inertia = 0.4

SCALE = math.sqrt(math.log2(math.e) / 4)
SOFT = 0.01 * SCALE * SCALE
LIFT = 2.0**SOFT
GAIN = LIFT * SCALE * stiffness
BOND = LIFT * SCALE * cohesion
DRAG = LIFT * stiffness


def iota(shape, dim):
    return lax.broadcasted_iota(I32, shape, dim)


def thirds(x):
    hi = x.astype(BF16).astype(F32)
    rest = x - hi
    mid = rest.astype(BF16).astype(F32)
    return jnp.concatenate([hi, mid, rest - mid], 0).astype(BF16)


def joined(y):
    n = y.shape[0] // 3
    return (y[2 * n :] + y[n : 2 * n]) + y[:n]


def dot(a, b):
    return lax.dot_general(a, b, (((1,), (0,)), ((), ())), preferred_element_type=F32)


def dot_t(a, b):
    return lax.dot_general(a, b, (((1,), (1,)), ((), ())), preferred_element_type=F32)


def hot(index, count):
    return jnp.where(iota((count, index.shape[1]), 0) == index, 1.0, 0.0).astype(BF16)


def wide(row):
    return jnp.concatenate([row, jnp.zeros((1, LANES - row.shape[1]), row.dtype)], 1)


def stack(rows, count):
    at = iota((count, rows[0].shape[1]), 0)
    out = jnp.zeros((count, rows[0].shape[1]), F32)
    for k, row in enumerate(rows):
        out = jnp.where(at == k, row, out)
    return out


def compact(actives, fields):
    segments = len(actives)
    flags = stack([a.astype(F32) for a in actives], 16)
    below = jnp.where(iota((LANES, LANES), 0) < iota((LANES, LANES), 1), 1.0, 0.0).astype(BF16)
    inside = dot(flags.astype(BF16), below)
    sums = dot(flags.astype(BF16), jnp.ones((LANES, LANES), BF16))
    ranks = []
    before = jnp.zeros((1, LANES), F32)
    for s in range(segments):
        ranks.append(jnp.where(actives[s], inside[s : s + 1] + before, -1.0).astype(I32))
        before = before + sums[s : s + 1]
    total = jnp.sum(flags).astype(I32)
    parts = thirds(jnp.concatenate([stack(f, 16) for f in fields], 1))
    return jnp.concatenate(ranks, 1), parts, total


def picked(ranks, parts, base, widths):
    at = iota((WIDTH, ranks.shape[1]), 0)
    want = base + jnp.where(at < LANES, at & (widths[0] - 1), LANES + (at & (widths[1] - 1)))
    chosen = jnp.where(want == ranks, 1.0, 0.0).astype(BF16)
    return joined(dot_t(parts, chosen))


def worlds(table_ref, pose):
    at = iota((4 * KINDS, pose.shape[1]), 0)
    kinds = jnp.where(((at & (KINDS - 1)) == pose[12:13].astype(I32)) & (at < 3 * KINDS), 1.0, 0.0).astype(BF16)
    shapes = dot(table_ref[...], kinds)
    offset = [shapes[e * SUB : (e + 1) * SUB] for e in range(4)]
    turn = [SCALE * pose[3 + n : 4 + n] for n in range(9)]
    return [
        turn[3 * c] * offset[0] + turn[3 * c + 1] * offset[1] + turn[3 * c + 2] * offset[2] for c in range(3)
    ] + [GAIN * offset[3]]


def interact(u, v_ref):
    def step(b, sums):
        v = [v_ref[c, pl.ds(b, 8, stride=0), :] for c in range(4)]
        out = []
        for one, s in zip(u, sums):
            x, y, z = (one[c] - v[c] for c in range(3))
            square = (x * x + SOFT) + y * y + z * z
            m = ((one[3] + v[3]) * lax.rsqrt(square) - DRAG) * jnp.exp2(-square)
            out.append((s[0] + m * x, s[1] + m * y, s[2] + m * z))
        return tuple(out)

    zero = jnp.zeros((8, LANES), F32)
    sums = lax.fori_loop(0, SUB, step, ((zero,) * 3,) * len(u), unroll=32)
    rows = [zero] * 6
    for one, g in zip(u, sums):
        for c in range(3):
            n, o = (c + 1) % 3, (c + 2) % 3
            rows[c] = rows[c] + g[c]
            rows[3 + c] = rows[3 + c] + (one[n] * g[o] - one[o] * g[n])
    return rows


def dealt(u_ref, width):
    rows = SUB * width // LANES
    part = iota((rows, LANES), 1) // width
    for c in range(4):
        value = u_ref[c, :rows, :]
        for h in range(1, LANES // width):
            value = jnp.where(part == h, u_ref[c, h * rows : (h + 1) * rows, :], value)
        u_ref[c, :rows, :] = value


def half_tile(width, u_ref, w_ref):
    def blocks(h, count):
        return [[u_ref[c, pl.ds(h * 32 + 8 * k, 8), :] for c in range(4)] for k in range(count)]

    for size in (64, 32, 16):
        pl.when(width == size)(functools.partial(dealt, u_ref, size))
    zero = (jnp.zeros((8, LANES), F32),) * 6

    def whole():
        def step(h, terms):
            return tuple(a + b for a, b in zip(terms, interact(blocks(h, 4), w_ref)))

        return lax.fori_loop(0, width // 32, step, zero)

    terms = lax.cond(width == 16, lambda: tuple(interact(blocks(0, 2), w_ref)), whole)
    return stack([jnp.sum(t, 0, keepdims=True) for t in terms], 8)


def prepare_kernel(
    position_hbm, velocity_hbm, accel_hbm, turn_hbm, kind_hbm, first_hbm, second_hbm, neck_hbm,
    cross_first_hbm, cross_second_hbm, cross_neck_hbm, export_hbm,
    moved_ref, thirds_ref, list_ref, near_ref, far1_ref, far2_ref, far3_ref,
    position_ref, velocity_ref, accel_ref, turn_ref, kind_ref, first_ref, second_ref, neck_ref,
    cross_first_ref, cross_second_ref, cross_neck_ref, export_ref, pose_ref, hot_ref, sems,
):
    sources = (
        position_hbm, velocity_hbm, accel_hbm, turn_hbm, kind_hbm, first_hbm, second_hbm, neck_hbm,
        cross_first_hbm, cross_second_hbm, cross_neck_hbm, export_hbm,
    )
    targets = (
        position_ref, velocity_ref, accel_ref, turn_ref, kind_ref, first_ref, second_ref, neck_ref,
        cross_first_ref, cross_second_ref, cross_neck_ref, export_ref,
    )
    copies = [pltpu.make_async_copy(a, b, sems.at[k]) for k, (a, b) in enumerate(zip(sources, targets))]
    for k in (5, 8, 11, 3, 0, 1, 2, 4, 6, 7, 9, 10):
        copies[k].start()
    group = lax.axis_index("group")
    for k in (5, 8, 11):
        copies[k].wait()
    index = jnp.concatenate([first_ref[...], wide(cross_first_ref[...]), export_ref[...]], 1)
    hot_ref[...] = hot(index, GRAINS_DEV)
    for k in (3, 0, 1, 2, 4, 6, 7, 9, 10):
        copies[k].wait()
    moved = position_ref[...] + time_step * velocity_ref[...] + 0.5 * time_step**2 * accel_ref[...]
    moved_ref[...] = moved
    pose_ref[0:3, :] = moved
    pose_ref[3:12, :] = turn_ref[...]
    pose_ref[12:13, :] = kind_ref[...].astype(F32)
    pose_ref[13:16, :] = jnp.zeros((3, GRAINS_DEV), F32)
    poses = thirds(pose_ref[...])
    thirds_ref[...] = poses
    got = joined(dot(poses, hot_ref[...]))
    at = iota((16, LANES), 0)
    second, neck = second_ref[...].astype(F32), neck_ref[...]
    cross_second, cross_neck = wide(cross_second_ref[...]).astype(F32), wide(cross_neck_ref[...])
    near_ref[0:16, :] = pose_ref[:, :BOUND_DEV]
    near_ref[16:32, :] = jnp.where(at == 14, neck, jnp.where(at == 13, second, got[:, :LANES]))
    listed = jnp.where(at == 14, cross_neck, jnp.where(at == 13, cross_second, got[:, LANES : 2 * LANES]))
    exported = got[:, 2 * LANES :]
    for k, far_ref in ((1, far1_ref), (2, far2_ref), (3, far3_ref)):
        to = (group + k) & 3
        turned = pltpu.roll(exported, (64 - CX * to) & (LANES - 1), 1)
        far_ref[...] = jnp.where(iota((16, LANES), 1) < 64, listed, turned)
    first, cross_first = first_ref[...].astype(F32), wide(cross_first_ref[...]).astype(F32)
    list_ref[...] = stack(
        [first, second, neck, cross_first, cross_second, cross_neck, export_ref[...].astype(F32)], 8
    )


def tiles(total, ranks, parts, other_of, poses_ref, table_ref, out_ref, work, both):
    u_ref, w_ref, terms_ref = work

    def tile(t, carry):
        left = total - t * WIDTH
        counts = [left - n * LANES for n in range(HALVES)]
        widths = [
            jnp.where(n <= 16, 16, jnp.where(n <= 32, 32, jnp.where(n <= 64, 64, LANES))).astype(I32) for n in counts
        ]
        fields = picked(ranks, parts, t * WIDTH, widths)
        own = hot(fields[0:1].astype(I32) - 1, GRAINS_DEV)
        mine = joined(dot(poses_ref[...], own))
        other = hot(fields[1:2].astype(I32) - 1, other_of.shape[1])
        theirs = joined(dot(other_of[...], other))
        shift = [SCALE * (mine[c : c + 1] - theirs[c : c + 1]) for c in range(3)]
        second = worlds(table_ref, theirs)
        first = worlds(table_ref, mine)
        first = [first[c] + shift[c] for c in range(3)] + [first[3] - BOND * fields[2:3]]
        for n in range(HALVES):
            for c in range(4):
                w_ref[n, c] = second[c][:, n * LANES : (n + 1) * LANES]
                u_ref[n, c] = first[c][:, n * LANES : (n + 1) * LANES]
        terms_ref[...] = jnp.zeros_like(terms_ref)

        def half(n, none):
            width = jnp.where(n == 0, widths[0], widths[1])
            terms_ref[n] = half_tile(width, u_ref.at[n], w_ref.at[n])
            return none

        lax.fori_loop(0, jnp.minimum(HALVES, (left + LANES - 1) // LANES), half, 0)
        terms = jnp.concatenate([terms_ref[n] for n in range(HALVES)], 1)
        force = [terms[c : c + 1] for c in range(3)]
        rows = [f * (1 / SCALE) for f in force]
        for c in range(3):
            n, o = (c + 1) % 3, (c + 2) % 3
            rows.append((terms[3 + c : 4 + c] - (shift[n] * force[o] - shift[o] * force[n])) * (1 / SCALE**2))
        found = joined(dot_t(thirds(stack(rows, 8)), own))
        if both:
            back = [-r for r in rows[:3]] + [terms[3 + c : 4 + c] * (-1 / SCALE**2) for c in range(3)]
            found = found + joined(dot_t(thirds(stack(back, 8)), other))
        out_ref[...] += found
        return carry

    lax.fori_loop(0, (total + WIDTH - 1) // WIDTH, tile, 0)


def listed(list_ref):
    rows = [list_ref[k : k + 1, :] for k in range(7)]
    return [row if k in (2, 5, 6) else row.astype(I32) for k, row in enumerate(rows)]


def local_kernel(
    poses_ref, list_ref, offset_ref, radius_ref,
    out_ref, table_ref,
    *work,
):
    group = lax.axis_index("group")
    blank = jnp.zeros((LANES - KINDS, SUB), F32)
    for e in range(4):
        rows = radius_ref[...] if e == 3 else offset_ref[:, e, :]
        hi = rows.astype(BF16).astype(F32)
        mid = (rows - hi).astype(BF16).astype(F32)
        low = rows - hi - mid
        table_ref[e * SUB : (e + 1) * SUB, :LANES] = jnp.concatenate([hi, mid], 0).T.astype(BF16)
        table_ref[e * SUB : (e + 1) * SUB, LANES:] = jnp.concatenate([low, blank], 0).T.astype(BF16)
    out_ref[...] = jnp.zeros_like(out_ref)
    first, second, neck, cross_first, cross, cross_neck, export = listed(list_ref)
    ours = (cross >> 5 == group) & (iota((1, LANES), 1) < 64)
    slot = joined(dot(thirds(stack([export], 16)), hot(cross, LANES)))[0:1]
    partner = (first + 1 + second) & (GRAINS_DEV - 1)
    ranks, parts, total = compact(
        [second < GRAINS_DEV - 1, ours],
        [
            [(first + 1).astype(F32), (partner + 1).astype(F32), neck],
            [(cross_first + 1).astype(F32), slot + 1, cross_neck],
        ],
    )
    tiles(total, ranks, parts, poses_ref, poses_ref, table_ref, out_ref, work, True)


def remote_kernel(
    poses_ref, list_ref, table_ref, local_ref, velocity_ref, accel_ref, spin_ref, before_ref, after_ref, far1_ref, far2_ref, far3_ref,
    velocity_out_ref, spin_out_ref,
    pool_ref, out_ref, *work,
):
    group = lax.axis_index("group")
    lane = iota((1, LANES), 1)
    fars = (far1_ref, far2_ref, far3_ref)
    pool = [before_ref[0:16, :], after_ref[0:16, :], before_ref[16:32, :], after_ref[16:32, :]]
    pool_ref[...] = thirds(jnp.concatenate(pool + [f[...] for f in fars], 1))
    out_ref[...] = local_ref[...]
    actives, fields = [], []

    def add(active, own, place, neck):
        actives.append(active)
        fields.append([(own + 1).astype(F32), (place + 1).astype(F32), neck])

    first, second, neck, cross_first, cross, cross_neck, export = listed(list_ref)
    beyond = second - (GRAINS_DEV - 1)
    add(beyond >= 0, first, beyond, neck)
    way = (group - (cross >> 5)) & 3
    add(
        (way != 0) & (lane < 64),
        cross_first,
        3 * LANES + way * LANES + 64 + (cross & (CX - 1)),
        cross_neck,
    )
    beyond = before_ref[29:30, :].astype(I32) - (GRAINS_DEV - 1)
    add(beyond >= BOUND_DEV, beyond - BOUND_DEV, 2 * LANES + lane, before_ref[30:31, :])
    beyond = after_ref[29:30, :].astype(I32) - (GRAINS_DEV - 1)
    add((beyond >= 0) & (beyond < BOUND_DEV), beyond, 3 * LANES + lane, after_ref[30:31, :])
    exports = thirds(stack([export], 16))
    for k in (1, 2, 3):
        wanted = fars[k - 1][13:14, :].astype(I32)
        sender = (group - k) & 3
        slot = joined(dot(exports, hot(sender * CX + (wanted & (CX - 1)), LANES)))[0:1]
        add(
            (wanted >> 5 == group) & (lane < 64),
            slot,
            (3 + k) * LANES + lane,
            fars[k - 1][14:15, :],
        )
    ranks, parts, total = compact(actives, fields)
    tiles(total, ranks, parts, pool_ref, poses_ref, table_ref, out_ref, work, False)
    velocity_out_ref[...] = velocity_ref[...] + 0.5 * time_step * (accel_ref[...] + out_ref[0:3, :])
    spin_out_ref[...] = spin_ref[...] + time_step * out_ref[3:6, :] / inertia


def shifted(array, axis, by):
    devices = lax.axis_size(axis)
    return lax.ppermute(array, axis, [(i, (i + by) % devices) for i in range(devices)])


def shape(rows, columns, kind=F32):
    return jax.ShapeDtypeStruct((rows, columns), kind)


def on_device(
    position, velocity, accel_old, orientation, spin, shape_index, shape_offsets, shape_radii,
    pair_first, pair_second, pair_neck, cross_first, cross_second, cross_neck, export_slots,
):
    row = lambda x: x.reshape(1, x.shape[0])
    sources = (position, velocity, accel_old, orientation) + tuple(
        row(x)
        for x in (
            shape_index, pair_first, pair_second, pair_neck, cross_first, cross_second, cross_neck, export_slots
        )
    )
    moved, poses, lists, near, far1, far2, far3 = pl.pallas_call(
        prepare_kernel,
        in_specs=[pl.BlockSpec(memory_space=pltpu.MemorySpace.HBM)] * 12,
        out_shape=(
            shape(3, GRAINS_DEV), shape(48, GRAINS_DEV, BF16), shape(8, LANES), shape(32, LANES),
            shape(16, LANES), shape(16, LANES), shape(16, LANES),
        ),
        scratch_shapes=[pltpu.VMEM(x.shape, x.dtype) for x in sources]
        + [pltpu.VMEM((16, GRAINS_DEV), F32), pltpu.VMEM((GRAINS_DEV, 3 * LANES), BF16), pltpu.SemaphoreType.DMA((12,))],
        compiler_params=pltpu.CompilerParams(vmem_limit_bytes=60 << 20),
        name="prepare",
    )(*sources)
    before = shifted(near, "region", 1)
    after = shifted(near, "region", -1)
    fars = [shifted(f, "group", k) for k, f in ((1, far1), (2, far2), (3, far3))]
    work = [
        pltpu.VMEM((HALVES, 4, SUB, LANES), F32),
        pltpu.VMEM((HALVES, 4, SUB, LANES), F32),
        pltpu.VMEM((HALVES, 8, LANES), F32),
    ]
    local, table = pl.pallas_call(
        local_kernel,
        out_shape=(shape(8, GRAINS_DEV), shape(4 * SUB, 4 * KINDS, BF16)),
        scratch_shapes=work,
        compiler_params=pltpu.CompilerParams(vmem_limit_bytes=32 << 20),
        cost_estimate=pl.CostEstimate(flops=4_000_000_000, bytes_accessed=1_000_000, transcendentals=4_000_000),
        name="local",
    )(poses, lists, shape_offsets, shape_radii)
    velocity_new, spin_new = pl.pallas_call(
        remote_kernel,
        out_shape=(shape(3, GRAINS_DEV), shape(3, GRAINS_DEV)),
        scratch_shapes=[
            pltpu.VMEM((48, 7 * LANES), BF16), pltpu.VMEM((8, GRAINS_DEV), F32)
        ] + work,
        compiler_params=pltpu.CompilerParams(vmem_limit_bytes=32 << 20),
        name="remote",
    )(poses, lists, table, local, velocity, accel_old, spin, before, after, *fars)
    return (moved, velocity_new, spin_new)


def solution(mesh):
    both = ("group", "region")
    wide_spec, flat = P(None, both), P(both)
    return jax.shard_map(
        on_device,
        mesh=mesh,
        in_specs=(wide_spec,) * 5 + (flat, P(), P()) + (flat,) * 7,
        out_specs=(wide_spec,) * 3,
        check_vma=False,
    )
```

```python
import functools
import math

import jax
import jax.numpy as jnp
from jax import lax
from jax.experimental import pallas as pl
from jax.experimental.pallas import tpu as pltpu
from jax.sharding import PartitionSpec as P

F32 = jnp.float32
BF16 = jnp.bfloat16
I32 = jnp.int32

BOUND_DEV = 128
CX = 32
KINDS = 64
SUB = 128
GRAINS_DEV = 1024
LANES = 128
HALVES = 2
WIDTH = HALVES * LANES

time_step = 0.05
stiffness = 0.0078125
cohesion = 0.05
inertia = 0.4

SCALE = math.sqrt(math.log2(math.e) / 4)
SOFT = 0.01 * SCALE * SCALE
LIFT = 2.0**SOFT
GAIN = LIFT * SCALE * stiffness
BOND = LIFT * SCALE * cohesion
DRAG = LIFT * stiffness


def iota(shape, dim):
    return lax.broadcasted_iota(I32, shape, dim)


def thirds(x):
    hi = x.astype(BF16).astype(F32)
    rest = x - hi
    mid = rest.astype(BF16).astype(F32)
    return jnp.concatenate([hi, mid, rest - mid], 0).astype(BF16)


def joined(y):
    n = y.shape[0] // 3
    return (y[2 * n :] + y[n : 2 * n]) + y[:n]


def dot(a, b):
    return lax.dot_general(a, b, (((1,), (0,)), ((), ())), preferred_element_type=F32)


def dot_t(a, b):
    return lax.dot_general(a, b, (((1,), (1,)), ((), ())), preferred_element_type=F32)


def hot(index, count):
    return jnp.where(iota((count, index.shape[1]), 0) == index, 1.0, 0.0).astype(BF16)


def wide(row):
    return jnp.concatenate([row, jnp.zeros((1, LANES - row.shape[1]), row.dtype)], 1)


def stack(rows, count):
    at = iota((count, rows[0].shape[1]), 0)
    out = jnp.zeros((count, rows[0].shape[1]), F32)
    for k, row in enumerate(rows):
        out = jnp.where(at == k, row, out)
    return out


def compact(actives, fields):
    segments = len(actives)
    flags = stack([a.astype(F32) for a in actives], 16)
    below = jnp.where(iota((LANES, LANES), 0) < iota((LANES, LANES), 1), 1.0, 0.0).astype(BF16)
    inside = dot(flags.astype(BF16), below)
    sums = dot(flags.astype(BF16), jnp.ones((LANES, LANES), BF16))
    ranks = []
    before = jnp.zeros((1, LANES), F32)
    for s in range(segments):
        ranks.append(jnp.where(actives[s], inside[s : s + 1] + before, -1.0).astype(I32))
        before = before + sums[s : s + 1]
    total = jnp.sum(flags).astype(I32)
    parts = thirds(jnp.concatenate([stack(f, 16) for f in fields], 1))
    return jnp.concatenate(ranks, 1), parts, total


def picked(ranks, parts, base, widths):
    at = iota((WIDTH, ranks.shape[1]), 0)
    want = base + jnp.where(at < LANES, at & (widths[0] - 1), LANES + (at & (widths[1] - 1)))
    chosen = jnp.where(want == ranks, 1.0, 0.0).astype(BF16)
    return joined(dot_t(parts, chosen))


def worlds(table_ref, pose):
    at = iota((4 * KINDS, pose.shape[1]), 0)
    kinds = jnp.where(((at & (KINDS - 1)) == pose[12:13].astype(I32)) & (at < 3 * KINDS), 1.0, 0.0).astype(BF16)
    shapes = dot(table_ref[...], kinds)
    offset = [shapes[e * SUB : (e + 1) * SUB] for e in range(4)]
    turn = [SCALE * pose[3 + n : 4 + n] for n in range(9)]
    return [
        turn[3 * c] * offset[0] + turn[3 * c + 1] * offset[1] + turn[3 * c + 2] * offset[2] for c in range(3)
    ] + [GAIN * offset[3]]


def interact(u, v_ref):
    def step(b, sums):
        v = [v_ref[c, pl.ds(b, 8, stride=0), :] for c in range(4)]
        out = []
        for one, s in zip(u, sums):
            x, y, z = (one[c] - v[c] for c in range(3))
            square = (x * x + SOFT) + y * y + z * z
            m = ((one[3] + v[3]) * lax.rsqrt(square) - DRAG) * jnp.exp2(-square)
            out.append((s[0] + m * x, s[1] + m * y, s[2] + m * z))
        return tuple(out)

    zero = jnp.zeros((8, LANES), F32)
    sums = lax.fori_loop(0, SUB, step, ((zero,) * 3,) * len(u), unroll=64)
    rows = [zero] * 6
    for one, g in zip(u, sums):
        for c in range(3):
            n, o = (c + 1) % 3, (c + 2) % 3
            rows[c] = rows[c] + g[c]
            rows[3 + c] = rows[3 + c] + (one[n] * g[o] - one[o] * g[n])
    return rows


def dealt(u_ref, width):
    rows = SUB * width // LANES
    part = iota((rows, LANES), 1) // width
    for c in range(4):
        value = u_ref[c, :rows, :]
        for h in range(1, LANES // width):
            value = jnp.where(part == h, u_ref[c, h * rows : (h + 1) * rows, :], value)
        u_ref[c, :rows, :] = value


def half_tile(width, u_ref, w_ref):
    def blocks(h, count):
        return [[u_ref[c, pl.ds(h * 32 + 8 * k, 8), :] for c in range(4)] for k in range(count)]

    for size in (64, 32, 16):
        pl.when(width == size)(functools.partial(dealt, u_ref, size))
    zero = (jnp.zeros((8, LANES), F32),) * 6

    def whole():
        def step(h, terms):
            return tuple(a + b for a, b in zip(terms, interact(blocks(h, 4), w_ref)))

        return lax.fori_loop(0, width // 32, step, zero)

    terms = lax.cond(width == 16, lambda: tuple(interact(blocks(0, 2), w_ref)), whole)
    return stack([jnp.sum(t, 0, keepdims=True) for t in terms], 8)


def prepare_kernel(
    position_hbm, velocity_hbm, accel_hbm, turn_hbm, kind_hbm, first_hbm, second_hbm, neck_hbm,
    cross_first_hbm, cross_second_hbm, cross_neck_hbm, export_hbm,
    moved_ref, thirds_ref, list_ref, near_ref, far1_ref, far2_ref, far3_ref,
    position_ref, velocity_ref, accel_ref, turn_ref, kind_ref, first_ref, second_ref, neck_ref,
    cross_first_ref, cross_second_ref, cross_neck_ref, export_ref, pose_ref, hot_ref, sems,
):
    sources = (
        position_hbm, velocity_hbm, accel_hbm, turn_hbm, kind_hbm, first_hbm, second_hbm, neck_hbm,
        cross_first_hbm, cross_second_hbm, cross_neck_hbm, export_hbm,
    )
    targets = (
        position_ref, velocity_ref, accel_ref, turn_ref, kind_ref, first_ref, second_ref, neck_ref,
        cross_first_ref, cross_second_ref, cross_neck_ref, export_ref,
    )
    copies = [pltpu.make_async_copy(a, b, sems.at[k]) for k, (a, b) in enumerate(zip(sources, targets))]
    for k in (5, 8, 11, 3, 0, 1, 2, 4, 6, 7, 9, 10):
        copies[k].start()
    group = lax.axis_index("group")
    for k in (5, 8, 11):
        copies[k].wait()
    index = jnp.concatenate([first_ref[...], wide(cross_first_ref[...]), export_ref[...]], 1)
    hot_ref[...] = hot(index, GRAINS_DEV)
    for k in (3, 0, 1, 2, 4, 6, 7, 9, 10):
        copies[k].wait()
    moved = position_ref[...] + time_step * velocity_ref[...] + 0.5 * time_step**2 * accel_ref[...]
    moved_ref[...] = moved
    pose_ref[0:3, :] = moved
    pose_ref[3:12, :] = turn_ref[...]
    pose_ref[12:13, :] = kind_ref[...].astype(F32)
    pose_ref[13:16, :] = jnp.zeros((3, GRAINS_DEV), F32)
    poses = thirds(pose_ref[...])
    thirds_ref[...] = poses
    got = joined(dot(poses, hot_ref[...]))
    at = iota((16, LANES), 0)
    second, neck = second_ref[...].astype(F32), neck_ref[...]
    cross_second, cross_neck = wide(cross_second_ref[...]).astype(F32), wide(cross_neck_ref[...])
    near_ref[0:16, :] = pose_ref[:, :BOUND_DEV]
    near_ref[16:32, :] = jnp.where(at == 14, neck, jnp.where(at == 13, second, got[:, :LANES]))
    listed = jnp.where(at == 14, cross_neck, jnp.where(at == 13, cross_second, got[:, LANES : 2 * LANES]))
    exported = got[:, 2 * LANES :]
    for k, far_ref in ((1, far1_ref), (2, far2_ref), (3, far3_ref)):
        to = (group + k) & 3
        turned = pltpu.roll(exported, (64 - CX * to) & (LANES - 1), 1)
        far_ref[...] = jnp.where(iota((16, LANES), 1) < 64, listed, turned)
    first, cross_first = first_ref[...].astype(F32), wide(cross_first_ref[...]).astype(F32)
    list_ref[...] = stack(
        [first, second, neck, cross_first, cross_second, cross_neck, export_ref[...].astype(F32)], 8
    )


def tiles(total, ranks, parts, other_of, poses_ref, table_ref, out_ref, work, both):
    u_ref, w_ref, terms_ref = work

    def tile(t, carry):
        left = total - t * WIDTH
        counts = [left - n * LANES for n in range(HALVES)]
        widths = [
            jnp.where(n <= 16, 16, jnp.where(n <= 32, 32, jnp.where(n <= 64, 64, LANES))).astype(I32) for n in counts
        ]
        fields = picked(ranks, parts, t * WIDTH, widths)
        own = hot(fields[0:1].astype(I32) - 1, GRAINS_DEV)
        mine = joined(dot(poses_ref[...], own))
        other = hot(fields[1:2].astype(I32) - 1, other_of.shape[1])
        theirs = joined(dot(other_of[...], other))
        shift = [SCALE * (mine[c : c + 1] - theirs[c : c + 1]) for c in range(3)]
        second = worlds(table_ref, theirs)
        first = worlds(table_ref, mine)
        first = [first[c] + shift[c] for c in range(3)] + [first[3] - BOND * fields[2:3]]
        for n in range(HALVES):
            for c in range(4):
                w_ref[n, c] = second[c][:, n * LANES : (n + 1) * LANES]
                u_ref[n, c] = first[c][:, n * LANES : (n + 1) * LANES]
        terms_ref[...] = jnp.zeros_like(terms_ref)

        def half(n, none):
            width = jnp.where(n == 0, widths[0], widths[1])
            terms_ref[n] = half_tile(width, u_ref.at[n], w_ref.at[n])
            return none

        lax.fori_loop(0, jnp.minimum(HALVES, (left + LANES - 1) // LANES), half, 0)
        terms = jnp.concatenate([terms_ref[n] for n in range(HALVES)], 1)
        force = [terms[c : c + 1] for c in range(3)]
        rows = [f * (1 / SCALE) for f in force]
        for c in range(3):
            n, o = (c + 1) % 3, (c + 2) % 3
            rows.append((terms[3 + c : 4 + c] - (shift[n] * force[o] - shift[o] * force[n])) * (1 / SCALE**2))
        found = joined(dot_t(thirds(stack(rows, 8)), own))
        if both:
            back = [-r for r in rows[:3]] + [terms[3 + c : 4 + c] * (-1 / SCALE**2) for c in range(3)]
            found = found + joined(dot_t(thirds(stack(back, 8)), other))
        out_ref[...] += found
        return carry

    lax.fori_loop(0, (total + WIDTH - 1) // WIDTH, tile, 0)


def listed(list_ref):
    rows = [list_ref[k : k + 1, :] for k in range(7)]
    return [row if k in (2, 5, 6) else row.astype(I32) for k, row in enumerate(rows)]


def local_kernel(
    poses_ref, list_ref, offset_ref, radius_ref,
    out_ref, table_ref,
    *work,
):
    group = lax.axis_index("group")
    blank = jnp.zeros((LANES - KINDS, SUB), F32)
    for e in range(4):
        rows = radius_ref[...] if e == 3 else offset_ref[:, e, :]
        hi = rows.astype(BF16).astype(F32)
        mid = (rows - hi).astype(BF16).astype(F32)
        low = rows - hi - mid
        table_ref[e * SUB : (e + 1) * SUB, :LANES] = jnp.concatenate([hi, mid], 0).T.astype(BF16)
        table_ref[e * SUB : (e + 1) * SUB, LANES:] = jnp.concatenate([low, blank], 0).T.astype(BF16)
    out_ref[...] = jnp.zeros_like(out_ref)
    first, second, neck, cross_first, cross, cross_neck, export = listed(list_ref)
    ours = (cross >> 5 == group) & (iota((1, LANES), 1) < 64)
    slot = joined(dot(thirds(stack([export], 16)), hot(cross, LANES)))[0:1]
    partner = (first + 1 + second) & (GRAINS_DEV - 1)
    ranks, parts, total = compact(
        [second < GRAINS_DEV - 1, ours],
        [
            [(first + 1).astype(F32), (partner + 1).astype(F32), neck],
            [(cross_first + 1).astype(F32), slot + 1, cross_neck],
        ],
    )
    tiles(total, ranks, parts, poses_ref, poses_ref, table_ref, out_ref, work, True)


def remote_kernel(
    poses_ref, list_ref, table_ref, local_ref, velocity_ref, accel_ref, spin_ref, before_ref, after_ref, far1_ref, far2_ref, far3_ref,
    velocity_out_ref, spin_out_ref,
    pool_ref, out_ref, *work,
):
    group = lax.axis_index("group")
    lane = iota((1, LANES), 1)
    fars = (far1_ref, far2_ref, far3_ref)
    pool = [before_ref[0:16, :], after_ref[0:16, :], before_ref[16:32, :], after_ref[16:32, :]]
    pool_ref[...] = thirds(jnp.concatenate(pool + [f[...] for f in fars], 1))
    out_ref[...] = local_ref[...]
    actives, fields = [], []

    def add(active, own, place, neck):
        actives.append(active)
        fields.append([(own + 1).astype(F32), (place + 1).astype(F32), neck])

    first, second, neck, cross_first, cross, cross_neck, export = listed(list_ref)
    beyond = second - (GRAINS_DEV - 1)
    add(beyond >= 0, first, beyond, neck)
    way = (group - (cross >> 5)) & 3
    add(
        (way != 0) & (lane < 64),
        cross_first,
        3 * LANES + way * LANES + 64 + (cross & (CX - 1)),
        cross_neck,
    )
    beyond = before_ref[29:30, :].astype(I32) - (GRAINS_DEV - 1)
    add(beyond >= BOUND_DEV, beyond - BOUND_DEV, 2 * LANES + lane, before_ref[30:31, :])
    beyond = after_ref[29:30, :].astype(I32) - (GRAINS_DEV - 1)
    add((beyond >= 0) & (beyond < BOUND_DEV), beyond, 3 * LANES + lane, after_ref[30:31, :])
    exports = thirds(stack([export], 16))
    for k in (1, 2, 3):
        wanted = fars[k - 1][13:14, :].astype(I32)
        sender = (group - k) & 3
        slot = joined(dot(exports, hot(sender * CX + (wanted & (CX - 1)), LANES)))[0:1]
        add(
            (wanted >> 5 == group) & (lane < 64),
            slot,
            (3 + k) * LANES + lane,
            fars[k - 1][14:15, :],
        )
    ranks, parts, total = compact(actives, fields)
    tiles(total, ranks, parts, pool_ref, poses_ref, table_ref, out_ref, work, False)
    velocity_out_ref[...] = velocity_ref[...] + 0.5 * time_step * (accel_ref[...] + out_ref[0:3, :])
    spin_out_ref[...] = spin_ref[...] + time_step * out_ref[3:6, :] / inertia


def shifted(array, axis, by):
    devices = lax.axis_size(axis)
    return lax.ppermute(array, axis, [(i, (i + by) % devices) for i in range(devices)])


def shape(rows, columns, kind=F32):
    return jax.ShapeDtypeStruct((rows, columns), kind)


def on_device(
    position, velocity, accel_old, orientation, spin, shape_index, shape_offsets, shape_radii,
    pair_first, pair_second, pair_neck, cross_first, cross_second, cross_neck, export_slots,
):
    row = lambda x: x.reshape(1, x.shape[0])
    sources = (position, velocity, accel_old, orientation) + tuple(
        row(x)
        for x in (
            shape_index, pair_first, pair_second, pair_neck, cross_first, cross_second, cross_neck, export_slots
        )
    )
    moved, poses, lists, near, far1, far2, far3 = pl.pallas_call(
        prepare_kernel,
        in_specs=[pl.BlockSpec(memory_space=pltpu.MemorySpace.HBM)] * 12,
        out_shape=(
            shape(3, GRAINS_DEV), shape(48, GRAINS_DEV, BF16), shape(8, LANES), shape(32, LANES),
            shape(16, LANES), shape(16, LANES), shape(16, LANES),
        ),
        scratch_shapes=[pltpu.VMEM(x.shape, x.dtype) for x in sources]
        + [pltpu.VMEM((16, GRAINS_DEV), F32), pltpu.VMEM((GRAINS_DEV, 3 * LANES), BF16), pltpu.SemaphoreType.DMA((12,))],
        compiler_params=pltpu.CompilerParams(vmem_limit_bytes=60 << 20),
        name="prepare",
    )(*sources)
    before = shifted(near, "region", 1)
    after = shifted(near, "region", -1)
    fars = [shifted(f, "group", k) for k, f in ((1, far1), (2, far2), (3, far3))]
    work = [
        pltpu.VMEM((HALVES, 4, SUB, LANES), F32),
        pltpu.VMEM((HALVES, 4, SUB, LANES), F32),
        pltpu.VMEM((HALVES, 8, LANES), F32),
    ]
    local, table = pl.pallas_call(
        local_kernel,
        out_shape=(shape(8, GRAINS_DEV), shape(4 * SUB, 4 * KINDS, BF16)),
        scratch_shapes=work,
        compiler_params=pltpu.CompilerParams(vmem_limit_bytes=32 << 20),
        cost_estimate=pl.CostEstimate(flops=4_000_000_000, bytes_accessed=1_000_000, transcendentals=4_000_000),
        name="local",
    )(poses, lists, shape_offsets, shape_radii)
    velocity_new, spin_new = pl.pallas_call(
        remote_kernel,
        out_shape=(shape(3, GRAINS_DEV), shape(3, GRAINS_DEV)),
        scratch_shapes=[
            pltpu.VMEM((48, 7 * LANES), BF16), pltpu.VMEM((8, GRAINS_DEV), F32)
        ] + work,
        compiler_params=pltpu.CompilerParams(vmem_limit_bytes=32 << 20),
        name="remote",
    )(poses, lists, table, local, velocity, accel_old, spin, before, after, *fars)
    return (moved, velocity_new, spin_new)


def solution(mesh):
    both = ("group", "region")
    wide_spec, flat = P(None, both), P(both)
    return jax.shard_map(
        on_device,
        mesh=mesh,
        in_specs=(wide_spec,) * 5 + (flat, P(), P()) + (flat,) * 7,
        out_specs=(wide_spec,) * 3,
        check_vma=False,
    )
```
